256 devices in a mesh: space: 64 (over z, x, core), tm: 4 (over y).
Axes of the slice: x: 4, y: 4, z: 8, core: 2. Of those that a mesh axis runs over, the one named last changes fastest.
Arguments:
- terminal: float32 [4, 64, 64, 8, 128], P('tm', None, 'space'), may hold values from -6 to 6
- goal_weight: float32 [64, 64, 8, 128], P(None, 'space'), may hold values from -4 to 4
- conduct: float32 [64, 8, 128], P('space'), may hold values from 0.02 to 0.16
- active_count: int32 [4], P('tm'), may hold values from 4 to 8
Outputs:
- basis: float32 [256, 65536], P('tm', 'space')
The draws below stay inside these ranges and needn't reach their ends.
Inputs may be any that keep to these rules, and one draw needn't show every extreme that they name: `active_count`: active layers count from the bottom of the embankment.
All inputs are finite; a program needn't handle non-finite values.
Results may differ from the reference program's by a relative error of at most 0.0001.
Values sent between devices are 32-bit elements; how exact they have to be, the bound alone decides.
A program may use at most 64 MiB of HBM per device.

```python
import math
import jax
import jax.numpy as jnp
from jax import lax

NY = 8
NZ = 128
GOALS = 64
STEPS = 4
LAYERS = 8
SIGN_STEPS = 2
NX = 64
NBLK = 4
N_TM = 4


def plant(values, rng, least, largest):
    extent = values.shape
    place = [jax.random.randint(jax.random.fold_in(rng, axis), (), 0, extent[axis]) for axis in range(len(extent))]
    values = values.at[tuple(place)].set(least)
    longest = extent.index(max(extent))
    place[longest] = (place[longest] + 1) % extent[longest]
    return values.at[tuple(place)].set(largest)


def steps_of(rng, shape, shards, low, top_value):
    def one(dim, blocks):
        draws = jax.random.uniform(jax.random.fold_in(jax.random.fold_in(rng, 6), dim), (blocks,), jnp.float32, low / len(shards), top_value / len(shards))
        return jnp.repeat(jnp.exp(draws), shape[dim] // blocks).reshape((-1,) + (1,) * (len(shape) - dim - 1))

    factor_of = one(*shards[0])
    for cut in shards[1:]:
        factor_of = factor_of * one(*cut)
    return factor_of


def noise(key, shape, deviation, limit, cuts=(), kind=jnp.bfloat16):
    array = deviation * jax.random.normal(key, shape, jnp.float32)
    if cuts:
        array = array * steps_of(key, shape, cuts, -0.22, 0.18)
    return jnp.clip(array, -limit, limit).astype(kind)


def setup_inputs(seed: int = 0) -> dict:
    splits = jax.random.split(jax.random.key(seed), 5)
    return {
        "terminal": noise(splits[0], (NBLK, GOALS, NX, NY, NZ), 1.0, 6.0, ((0, 4), (2, 64)), jnp.float32),
        "goal_weight": noise(splits[1], (GOALS, NX, NY, NZ), 0.5, 4.0, ((1, 64),), jnp.float32),
        "conduct": jnp.clip(jnp.exp(math.log(0.16) - 2.0794415 * jax.random.uniform(splits[2], (NX, NY, NZ), jnp.float32) ** steps_of(splits[2], (NX, NY, NZ), ((0, 64),), -0.2, 0.2)), 0.02, 0.16),
        "active_count": plant(jax.random.randint(splits[3], (NBLK,), LAYERS // 2, LAYERS + 1), jax.random.fold_in(splits[3], 1), LAYERS // 2, LAYERS).astype(jnp.int32),
    }


def product(left, right):
    return jnp.dot(left, right, precision=lax.Precision.HIGHEST)

def outer_gram(rows):
    return lax.dot_general(rows, rows, (((1,), (1,)), ((), ())), precision=lax.Precision.HIGHEST)

def filter_weights(gram_matrix):
    order_size = gram_matrix.shape[0]
    half_size = order_size // 2
    identity = jnp.eye(order_size, dtype=jnp.float32)
    energy = jnp.trace(gram_matrix) / order_size + 1e-06
    shifted = gram_matrix / energy - identity
    sign_iter = shifted / jnp.sqrt(jnp.sum(shifted * shifted) + 1e-06)
    for repeat in range(SIGN_STEPS):
        sign_iter = 0.5 * product(sign_iter, 3.0 * identity - product(sign_iter, sign_iter))
    keep_part = 0.5 * (identity + sign_iter)
    weights = (keep_part[:, :half_size] + keep_part[:, half_size:]) * (1.0 / jnp.sqrt(jnp.float32(2.0)))
    kept_energy = jnp.sum(weights * product(gram_matrix, weights))
    return weights * jnp.sqrt(energy * half_size / (kept_energy + 1e-06))

def merge_pair(lower_panel, upper_panel):
    stacked = jnp.concatenate([lower_panel, upper_panel], 0)
    weights = filter_weights(outer_gram(stacked))
    return lax.dot_general(weights, stacked, (((0,), (0,)), ((), ())), precision=lax.Precision.HIGHEST)

def neighbours(padded):
    total = padded[:, 2:, 1:-1, 1:-1] + padded[:, :-2, 1:-1, 1:-1]
    total = total + padded[:, 1:-1, 2:, 1:-1] + padded[:, 1:-1, :-2, 1:-1]
    total = total + padded[:, 1:-1, 1:-1, 2:] + padded[:, 1:-1, 1:-1, :-2]
    return total

def leaf_panel(block_index, terminal, goal_weight, conduct, active_count):
    depth = terminal.shape[4]
    layer_index = jnp.arange(depth) // (depth // LAYERS)
    active_mask = (layer_index < active_count[block_index]).astype(jnp.float32)
    adjoint_field = terminal[block_index] * active_mask
    snapshots = []
    for repeat in range(STEPS):
        padded = jnp.pad(adjoint_field, ((0, 0), (1, 1), (1, 1), (1, 1)))
        adjoint_field = active_mask * (adjoint_field + conduct * (neighbours(padded) - 6.0 * adjoint_field) + goal_weight)
        snapshots.append(adjoint_field.reshape(adjoint_field.shape[0], -1))
    return jnp.concatenate(snapshots, 0)

def merge_tree(first_block, span_count, terminal, goal_weight, conduct, active_count):
    if span_count == 1:
        return leaf_panel(first_block, terminal, goal_weight, conduct, active_count)
    half_span = span_count // 2
    lower_panel = merge_tree(first_block, half_span, terminal, goal_weight, conduct, active_count)
    upper_panel = merge_tree(first_block + half_span, half_span, terminal, goal_weight, conduct, active_count)
    return merge_pair(lower_panel, upper_panel)

def reference(terminal, goal_weight, conduct, active_count):
    return merge_tree(0, N_TM, terminal, goal_weight, conduct, active_count)
```

```python
import jax
import jax.numpy as jnp
from jax import lax
from jax.experimental import pallas as pl
from jax.experimental.pallas import tpu as pltpu
from jax.sharding import PartitionSpec as P

STEPS = 4
GOALS = 64
LAYERS = 8
NX_CHIPS = 4
N_TM = 4
CHUNKS = 2
F32 = jnp.float32
BF16 = jnp.bfloat16


def split(x):
    high = x.astype(BF16)
    return high, (x - high.astype(F32)).astype(BF16)


def dot(a, b, dims):
    return lax.dot_general(a, b, (dims, ((), ())), preferred_element_type=F32)


def dot3(ah, al, bh, bl, dims=((1,), (0,))):
    return dot(ah, bh, dims) + (dot(ah, bl, dims) + dot(al, bh, dims))


NT = ((1,), (1,))


class Links:
    def __init__(self, send_sems, recv_sems):
        self.send_sems, self.recv_sems, self.copies = send_sems, recv_sems, []

    def start(self, src, dst, device):
        n = len(self.copies)
        copy = pltpu.make_async_remote_copy(
            src_ref=src, dst_ref=dst, send_sem=self.send_sems.at[n], recv_sem=self.recv_sems.at[n],
            device_id=device, device_id_type=pl.DeviceIdType.MESH)
        copy.start()
        self.copies.append(copy)
        return copy

    def finish(self):
        for copy in self.copies:
            copy.wait_send()


def rows(start, size):
    return pl.ds(pl.multiple_of(start, 8), size)


def kernel(n_space, term_ref, goal_ref, cond_ref, count_ref, out_ref,
           field, goal, halo_l, halo_r, own, other, sh, sl,
           pg, pc, rx1, ry1, qx1, qy1, rx2, ry2, qz, rz, fz, q2x, q2y, gf,
           cx1, cy1, dx1, dy1, cx2, cy2, ez, crz, cfz, d2x, d2y, cb,
           gmat, s0f, s0h, s0l, zh, zl, s1h, s1l, ff, fh, fl, th, tl, wf, wh, wl, wt,
           wb, hb, mh, ml, g2, bs, send_sems, recv_sems):
    s = lax.axis_index("space")
    t = lax.axis_index("tm")
    core = s % 2
    chip = s // 2
    cx = chip % NX_CHIPS
    cz = chip // NX_CHIPS
    n_z = n_space // (2 * NX_CHIPS)
    left = (lax.rem(s + n_space - 1, n_space), t)
    right = (lax.rem(s + 1, n_space), t)
    partner = (s + 1 - 2 * core, t)

    def y_peer(d):
        return lax.rem(t + d, N_TM)

    def x_peer(d):
        return lax.rem(cx + d, NX_CHIPS)

    def z_peer(d):
        return lax.rem(cz + d, n_z)

    def at_y(d):
        return (s, y_peer(d))

    def at_x(d):
        return ((cz * NX_CHIPS + x_peer(d)) * 2 + core, t)

    def at_z(d):
        return ((z_peer(d) * NX_CHIPS + cx) * 2 + core, t)

    peers = [left, right] + [at_y(d) for d in range(1, N_TM)] + [at_x(d) for d in range(1, NX_CHIPS)]
    peers += [at_z(d) for d in range(1, n_z)]
    barrier = pltpu.get_barrier_semaphore()
    for peer in peers:
        pl.semaphore_signal(barrier, inc=1, device_id=peer, device_id_type=pl.DeviceIdType.MESH)

    lane = lax.broadcasted_iota(jnp.int32, (1, 128), 1)
    mask = (lane // (128 // LAYERS) < count_ref[0]).astype(F32)
    for y in range(8):
        field[0, y] = term_ref[pl.ds(y, GOALS, stride=8), :] * mask
        goal[y] = goal_ref[pl.ds(y, GOALS, stride=8), :] * mask
    pl.semaphore_wait(barrier, len(peers))

    links = Links(send_sems, recv_sems)
    size = GOALS // CHUNKS

    def part(c):
        return pl.ds(c * size, size)

    def send_halo(k, c):
        to_right = links.start(field.at[k, :, part(c)], halo_l.at[k, :, part(c)], right)
        to_left = links.start(field.at[k, :, part(c)], halo_r.at[k, :, part(c)], left)
        return to_right, to_left

    has_left = jnp.where(s > 0, 1.0, 0.0).astype(F32)
    has_right = jnp.where(s < n_space - 1, 1.0, 0.0).astype(F32)
    inner_lo = (lane > 0).astype(F32)
    inner_hi = (lane < 127).astype(F32)
    halos = {(0, c): send_halo(0, c) for c in range(CHUNKS)}
    spread = {}

    def absorb(k):
        for ref, base in ((own, 0), (other, 256)):
            for yy in range(2):
                for b in range(N_TM):
                    high, low = split(ref[k, yy, pl.ds(b * GOALS, GOALS), :])
                    sh[b, pl.ds(k * GOALS, GOALS), pl.ds(base + yy * 128, 128)] = high
                    sl[b, pl.ds(k * GOALS, GOALS), pl.ds(base + yy * 128, 128)] = low

    shared = {}
    for k in range(STEPS):
        for c in range(CHUNKS):
            for copy in halos[k, c]:
                copy.wait_recv()
            for y in range(8):
                here = field[k, y, part(c)]
                total = halo_l[k, y, part(c)] * has_left + halo_r[k, y, part(c)] * has_right
                if y > 0:
                    total = total + field[k, y - 1, part(c)]
                if y < 7:
                    total = total + field[k, y + 1, part(c)]
                total = total + pltpu.roll(here, 1, 1) * inner_lo + pltpu.roll(here, 127, 1) * inner_hi
                kappa = cond_ref[pl.ds(y, 1), :]
                field[k + 1, y, part(c)] = mask * (
                    here + kappa * (total - 6.0 * here)) + goal[y, part(c)]
            if k + 1 < STEPS:
                halos[k + 1, c] = send_halo(k + 1, c)
            spread[k, c] = [
                links.start(field.at[k + 1, pl.ds(2 * y_peer(d), 2), part(c)],
                            own.at[k, :, rows(t * GOALS + c * size, size)], at_y(d))
                for d in range(1, N_TM)]
            own[k, :, rows(t * GOALS + c * size, size)] = field[k + 1, pl.ds(2 * t, 2), part(c)]
        if k > 0:
            shared[k - 1] = share(links, spread, own, other, k - 1, partner)
    shared[STEPS - 1] = share(links, spread, own, other, STEPS - 1, partner)
    for k in range(STEPS):
        shared[k].wait_recv()
        absorb(k)

    lower, upper = 2 * core, 2 * core + 1

    def gram(i, j):
        return dot3(sh[i], sl[i], sh[j], sl[j], NT)

    for n, (i, j) in enumerate(((lower, lower), (lower, upper), (upper, upper))):
        g = gram(i, j)
        pg[pl.ds(n * 512, 256)] = g[:, :128]
        pg[pl.ds(n * 512 + 256, 256)] = g[:, 128:]
    for n, j in enumerate((2, 3)):
        g = gram(core, j)
        pc[pl.ds(n * 512, 256)] = g[:, :128]
        pc[pl.ds(n * 512 + 256, 256)] = g[:, 128:]

    def scatter(src, base, land, length, peer, at, count):
        return [links.start(src.at[rows(base + peer(d) * length, length)], land.at[d - 1], at(d))
                for d in range(1, count)]

    def reduced(src, base, land, length, copies, place):
        total = src[rows(base + place * length, length)]
        for d, copy in enumerate(copies):
            copy.wait_recv()
            total = total + land[d]
        return total

    def gather(src, dst, base, length, place, at, count):
        return [links.start(src, dst.at[rows(base + place * length, length)], at(d)) for d in range(1, count)]

    def wait(copies):
        for copy in copies:
            copy.wait_recv()

    def stage1(src, landx, landy):
        half = src.shape[0] // 2
        return (scatter(src, 0, landx, half // 4, x_peer, at_x, NX_CHIPS),
                scatter(src, half, landy, half // 4, y_peer, at_y, N_TM))

    def stage2(src, landx, landy, copies, qx, qy, landx2, landy2):
        half = src.shape[0] // 2
        qx[...] = reduced(src, 0, landx, half // 4, copies[0], cx)
        first = scatter(qx, 0, landx2, half // 16, y_peer, at_y, N_TM)
        qy[...] = reduced(src, half, landy, half // 4, copies[1], t)
        return first, scatter(qy, 0, landy2, half // 16, x_peer, at_x, NX_CHIPS)

    def stage3(qx, qy, landx2, landy2, copies, q, land):
        length = qx.shape[0] // 4
        q[pl.ds(0, length)] = reduced(qx, 0, landx2, length, copies[0], t)
        q[pl.ds(length, length)] = reduced(qy, 0, landy2, length, copies[1], cx)
        if q.shape[0] > 2 * length:
            q[pl.ds(2 * length, q.shape[0] - 2 * length)] = jnp.zeros((q.shape[0] - 2 * length, 128), F32)
        return scatter(q, 0, land, q.shape[0] // n_z, z_peer, at_z, n_z)

    def back1(q, land, copies, full):
        length = q.shape[0] // n_z
        full[rows(cz * length, length)] = reduced(q, 0, land, length, copies, cz)
        return gather(full.at[rows(cz * length, length)], full, 0, length, cz, at_z, n_z)

    def back2(full, copies, qx, qy):
        wait(copies)
        length = qx.shape[0] // 4
        first = gather(full.at[pl.ds(0, length)], qx, 0, length, t, at_y, N_TM)
        second = gather(full.at[pl.ds(length, length)], qy, 0, length, cx, at_x, NX_CHIPS)
        qx[rows(t * length, length)] = full[pl.ds(0, length)]
        qy[rows(cx * length, length)] = full[pl.ds(length, length)]
        return first, second

    def back3(qx, qy, copies, dst):
        length = qx.shape[0]
        wait(copies[0])
        first = gather(qx, dst, 0, length, cx, at_x, NX_CHIPS)
        wait(copies[1])
        second = gather(qy, dst, 4 * length, length, t, at_y, N_TM)
        dst[rows(cx * length, length)] = qx[...]
        dst[rows(4 * length + t * length, length)] = qy[...]
        return first + second

    g1 = stage1(pg, rx1, ry1)
    g2c = stage2(pg, rx1, ry1, g1, qx1, qy1, rx2, ry2)
    c1 = stage1(pc, cx1, cy1)
    g3 = stage3(qx1, qy1, rx2, ry2, g2c, qz, rz)
    c2 = stage2(pc, cx1, cy1, c1, dx1, dy1, cx2, cy2)
    g4 = back1(qz, rz, g3, fz)
    g5 = back2(fz, g4, q2x, q2y)
    c3 = stage3(dx1, dy1, cx2, cy2, c2, ez, crz)
    g6 = back3(q2x, q2y, g5, gf)
    c4 = back1(ez, crz, c3, cfz)
    wait(g6)

    cmat = cb.at[core]

    def eye(size):
        return (lax.broadcasted_iota(jnp.int32, (size, size), 0)
                == lax.broadcasted_iota(jnp.int32, (size, size), 1)).astype(F32)

    def block(ref, n):
        return jnp.concatenate([ref[pl.ds(n * 512, 256)], ref[pl.ds(n * 512 + 256, 256)]], 1)

    upper_right = block(gf, 1)
    gmat[pl.ds(0, 256), pl.ds(0, 256)] = block(gf, 0)
    gmat[pl.ds(0, 256), pl.ds(256, 256)] = upper_right
    gmat[pl.ds(256, 256), pl.ds(0, 256)] = upper_right.T
    gmat[pl.ds(256, 256), pl.ds(256, 256)] = block(gf, 2)

    def weights(between):
        identity = eye(256)
        trace = jnp.sum(gmat[pl.ds(0, 256), pl.ds(0, 256)] * identity) + jnp.sum(
            gmat[pl.ds(256, 256), pl.ds(256, 256)] * identity)
        energy = trace / 512.0 + 1e-6
        inverse = 1.0 / energy
        norm2 = jnp.float32(0.0)
        for i in range(2):
            for j in range(2):
                part_ = gmat[pl.ds(256 * i, 256), pl.ds(256 * j, 256)] * inverse
                if i == j:
                    part_ = part_ - identity
                s0f[pl.ds(256 * i, 256), pl.ds(256 * j, 256)] = part_
                norm2 = norm2 + jnp.sum(part_ * part_)
        norm = jnp.sqrt(norm2 + 1e-6)
        scale = 1.0 / norm
        for i in range(2):
            r = pl.ds(256 * i, 256)
            value = s0f[r] * scale
            s0f[r] = value
            s0h[r], s0l[r] = split(value)
        between(0)
        for i in range(2):
            r = pl.ds(256 * i, 256)
            zh[r], zl[r] = split(dot3(s0h[r], s0l[r], s0h[...], s0l[...]))
        between(1)
        for i in range(2):
            r = pl.ds(256 * i, 256)
            s1 = 1.5 * s0f[r] - 0.5 * dot3(s0h[r], s0l[r], zh[...], zl[...])
            s1h[r], s1l[r] = split(s1)
            f = s1[:, :256] + s1[:, 256:]
            ff[r] = f
            fh[r], fl[r] = split(f)
        between(2)
        for i in range(2):
            r = pl.ds(256 * i, 256)
            th[r], tl[r] = split(dot3(s1h[r], s1l[r], fh[...], fl[...]))
        for i in range(2):
            r = pl.ds(256 * i, 256)
            u = dot3(s1h[r], s1l[r], th[...], tl[...])
            w = (identity + 1.5 * ff[r] - 0.5 * u) * (0.5 / 2.0 ** 0.5)
            wf[r] = w
            wh[r], wl[r] = split(w)
        between(3)
        kept = jnp.float32(0.0)
        for i in range(2):
            r = pl.ds(256 * i, 256)
            gw = wf[r] + norm * dot3(s0h[r], s0l[r], wh[...], wl[...])
            ff[r] = gw
            kept = kept + jnp.sum(wf[r] * gw)
        ratio = 256.0 * energy / (energy * kept + 1e-6)
        alpha = jnp.sqrt(energy * ratio / energy)
        return energy, alpha

    state = {}

    def between(n):
        if n == 0:
            state["c5"] = back2(cfz, c4, d2x, d2y)
        if n == 1:
            state["c6"] = back3(d2x, d2y, state["c5"], cmat)
        if n == 2:
            wait(state["c6"])
            state["c7"] = links.start(cmat, cmat, partner)

    energy, alpha = weights(between)
    for i in range(2):
        wf[pl.ds(256 * i, 256)] = wf[pl.ds(256 * i, 256)] * alpha
    wb[core] = wf[...]
    send_w = links.start(wb.at[core], wb.at[core], partner)
    for i in range(2):
        fh[pl.ds(256 * i, 256)], fl[pl.ds(256 * i, 256)] = split(ff[pl.ds(256 * i, 256)])
    wt[...] = wf[...].T
    ah, al = split(wt[...])
    hb[core] = (energy * alpha) * dot3(ah, al, fh[...], fl[...])
    send_h = links.start(hb.at[core], hb.at[core], partner)
    state["c7"].wait_recv()
    send_w.wait_recv()

    w1h, w1l = split(wb[1])
    th[...] = w1h
    tl[...] = w1l
    for i in range(2):
        r = pl.ds(256 * i, 256)
        ch, cl = split(jnp.concatenate([cb[i, pl.ds(256 * j, 256)] for j in range(4)], 1))
        fh[r], fl[r] = split(dot3(ch, cl, th[...], tl[...]))
    for p in range(2):
        ah, al = split(wb[p].T)
        if p == 0:
            cross = dot3(ah, al, fh[...], fl[...])
            gmat[pl.ds(0, 256), pl.ds(256, 256)] = cross
            gmat[pl.ds(256, 256), pl.ds(0, 256)] = cross.T
        for i in range(2):
            block_h = sh[2 * p + i, :, pl.ds(0, 256)]
            block_l = sl[2 * p + i, :, pl.ds(0, 256)]
            term = dot3(ah[:, 256 * i:256 * i + 256], al[:, 256 * i:256 * i + 256], block_h, block_l)
            merged = term if i == 0 else merged + term
        mh[pl.ds(256 * p, 256)], ml[pl.ds(256 * p, 256)] = split(merged)
    send_h.wait_recv()
    gmat[pl.ds(0, 256), pl.ds(0, 256)] = hb[0]
    gmat[pl.ds(256, 256), pl.ds(256, 256)] = hb[1]
    _, alpha = weights(lambda n: None)
    ah, al = split(wf[...].T)
    bs[...] = alpha * dot3(ah, al, mh[...], ml[...])
    columns = pl.ds(pl.multiple_of(t * 256, 256), 256)
    final = [links.start(bs.at[rows(y_peer(d) * 64, 64)], out_ref.at[:, columns], at_y(d)) for d in range(1, N_TM)]
    out_ref[:, columns] = bs[rows(t * 64, 64)]
    wait(final)
    links.finish()


def share(links, spread, own, other, k, partner):
    for c in range(CHUNKS):
        for copy in spread[k, c]:
            copy.wait_recv()
    return links.start(own.at[k], other.at[k], partner)


def shards(terminal, goal_weight, conduct, active_count):
    n_space = lax.axis_size("space")
    n_z = n_space // (2 * NX_CHIPS)

    def f(*shape):
        return pltpu.VMEM(shape, F32)

    def h(*shape):
        return pltpu.VMEM(shape, BF16)

    scratch = [
        f(STEPS + 1, 8, GOALS, 128), f(8, GOALS, 128), f(STEPS, 8, GOALS, 128), f(STEPS, 8, GOALS, 128),
        f(STEPS, 2, 256, 128), f(STEPS, 2, 256, 128), h(4, 256, 512), h(4, 256, 512),
        f(1536, 128), f(1024, 128),
        f(3, 192, 128), f(3, 192, 128), f(192, 128), f(192, 128), f(3, 48, 128), f(3, 48, 128),
        f(128, 128), f(n_z - 1, 128 // n_z, 128), f(128, 128), f(192, 128), f(192, 128), f(1536, 128),
        f(3, 128, 128), f(3, 128, 128), f(128, 128), f(128, 128), f(3, 32, 128), f(3, 32, 128),
        f(64, 128), f(n_z - 1, 64 // n_z, 128), f(64, 128), f(128, 128), f(128, 128), f(2, 1024, 128),
        f(512, 512), f(512, 512), h(512, 512), h(512, 512), h(512, 512), h(512, 512), h(512, 512), h(512, 512),
        f(512, 256), h(512, 256), h(512, 256), h(512, 256), h(512, 256), f(512, 256), h(512, 256), h(512, 256),
        f(256, 512), f(2, 512, 256), f(2, 256, 256), h(512, 256), h(512, 256), f(8, 128), f(256, 256),
        pltpu.SemaphoreType.DMA((128,)), pltpu.SemaphoreType.DMA((128,)),
    ]
    vmem = pl.BlockSpec(memory_space=pltpu.VMEM)

    def body(*refs):
        kernel(n_space, *refs)

    return pl.pallas_call(
        body,
        out_shape=jax.ShapeDtypeStruct((256 // N_TM, 1024), F32),
        in_specs=[vmem, vmem, vmem, pl.BlockSpec(memory_space=pltpu.SMEM)],
        out_specs=vmem,
        scratch_shapes=scratch,
        compiler_params=pltpu.CompilerParams(
            collective_id=0, has_side_effects=True, vmem_limit_bytes=56 * 1024 * 1024),
        name="merge_tree",
    )(terminal.reshape(GOALS * 8, 128), goal_weight.reshape(GOALS * 8, 128), conduct.reshape(8, 128), active_count)


def solution(mesh):
    placed = (
        P("tm", None, "space", None, None),
        P(None, "space", None, None),
        P("space", None, None),
        P("tm"),
    )
    return jax.shard_map(
        shards, mesh=mesh, in_specs=placed, out_specs=P("tm", "space"), check_vma=False
    )
```

```python
import jax
import jax.numpy as jnp
from jax import lax
from jax.experimental import pallas as pl
from jax.experimental.pallas import tpu as pltpu
from jax.sharding import PartitionSpec as P

STEPS = 4
GOALS = 64
LAYERS = 8
NX_CHIPS = 4
N_TM = 4
CHUNKS = 4
F32 = jnp.float32
BF16 = jnp.bfloat16


def split(x):
    high = x.astype(BF16)
    return high, (x - high.astype(F32)).astype(BF16)


def dot(a, b, dims):
    return lax.dot_general(a, b, (dims, ((), ())), preferred_element_type=F32)


def dot3(ah, al, bh, bl, dims=((1,), (0,))):
    return dot(ah, bh, dims) + (dot(ah, bl, dims) + dot(al, bh, dims))


NT = ((1,), (1,))


class Arrival:
    def __init__(self, sem, whole):
        self.sem, self.whole, self.done = sem, whole, False

    def wait(self):
        self.done = True
        pltpu.make_async_copy(self.whole, self.whole, self.sem).wait()


class Links:
    def __init__(self, send_sems, recv_sems):
        self.send_sems, self.recv_sems, self.sent, self.arrivals = send_sems, recv_sems, [], []

    def sending(self, whole):
        sem = self.send_sems.at[len(self.sent)]
        self.sent.append(Arrival(sem, whole))
        return sem

    def arrival(self, whole):
        arrival = Arrival(self.recv_sems.at[len(self.arrivals)], whole)
        self.arrivals.append(arrival)
        return arrival

    def group(self, copies, whole, send_sem=None):
        if send_sem is None:
            send_sem = self.sending(whole)
        arrival = self.arrival(whole)
        for src, dst, device in copies:
            self.copy(src, dst, device, send_sem, arrival)
        return arrival

    def copy(self, src, dst, device, send_sem, arrival):
        pltpu.make_async_remote_copy(
            src_ref=src, dst_ref=dst, send_sem=send_sem, recv_sem=arrival.sem,
            device_id=device, device_id_type=pl.DeviceIdType.MESH).start()

    def finish(self):
        for sent in self.sent:
            sent.wait()


def rows(start, size):
    return pl.ds(pl.multiple_of(start, 8), size)


def kernel(n_space, term_ref, goal_ref, cond_ref, count_ref, out_ref,
           term_raw, goal_raw, in_sems, field, goal, halo, own, other, sh, sl,
           pg, pc, rx1, ry1, qx1, qy1, rx2, ry2, qz, rz, fz, q2x, q2y, gf,
           cx1, cy1, dx1, dy1, cx2, cy2, ez, crz, cfz, d2x, d2y, cb,
           gmat, s0f, s0h, s0l, zh, zl, s1h, s1l, ff, fh, fl, th, tl, wf, wh, wl, wt,
           wb, hb, mh, ml, bs, send_sems, recv_sems):
    s = lax.axis_index("space")
    t = lax.axis_index("tm")
    core = s % 2
    chip = s // 2
    cx = chip % NX_CHIPS
    cz = chip // NX_CHIPS
    n_z = n_space // (2 * NX_CHIPS)
    left = (lax.rem(s + n_space - 1, n_space), t)
    right = (lax.rem(s + 1, n_space), t)
    partner = (s + 1 - 2 * core, t)

    def y_peer(d):
        return lax.rem(t + d, N_TM)

    def x_peer(d):
        return lax.rem(cx + d, NX_CHIPS)

    def z_peer(d):
        return lax.rem(cz + d, n_z)

    def at_y(d):
        return (s, y_peer(d))

    def at_x(d):
        return ((cz * NX_CHIPS + x_peer(d)) * 2 + core, t)

    def at_z(d):
        return ((z_peer(d) * NX_CHIPS + cx) * 2 + core, t)

    peers = [left, right] + [at_y(d) for d in range(1, N_TM)] + [at_x(d) for d in range(1, NX_CHIPS)]
    peers += [at_z(d) for d in range(1, n_z)]
    barrier = pltpu.get_barrier_semaphore()
    for peer in peers:
        pl.semaphore_signal(barrier, inc=1, device_id=peer, device_id_type=pl.DeviceIdType.MESH)

    size = GOALS // CHUNKS
    loads = [pltpu.make_async_copy(term_ref, term_raw, in_sems.at[0]),
             pltpu.make_async_copy(goal_ref, goal_raw, in_sems.at[1])]
    for load in loads:
        load.start()
    lane = lax.broadcasted_iota(jnp.int32, (1, 128), 1)
    mask = (lane // (128 // LAYERS) < count_ref[0]).astype(F32)
    loads[0].wait()
    for y in range(8):
        for c in range(CHUNKS):
            field[0, c, y] = term_raw[pl.ds(c * size * 8 + y, size, stride=8), :] * mask
    pl.semaphore_wait(barrier, len(peers))

    links = Links(send_sems, recv_sems)

    halo_sem = links.sending(halo)
    spread_sem = links.sending(own.at[:, pl.ds(0, N_TM - 1)])
    share_sem = links.sending(own)

    def send_halo(k, c):
        return links.group([(field.at[k, c], halo.at[k, c, 0], right), (field.at[k, c], halo.at[k, c, 1], left)],
                           halo.at[k, c], halo_sem)

    has_left = jnp.where(s > 0, 1.0, 0.0).astype(F32)
    has_right = jnp.where(s < n_space - 1, 1.0, 0.0).astype(F32)
    inner_lo = (lane > 0).astype(F32)
    inner_hi = (lane < 127).astype(F32)
    halos = {(0, c): send_halo(0, c) for c in range(CHUNKS)}
    loads[1].wait()
    for y in range(8):
        for c in range(CHUNKS):
            goal[c, y] = goal_raw[pl.ds(c * size * 8 + y, size, stride=8), :] * mask
    spread = [links.arrival(own.at[k, pl.ds(0, N_TM - 1)]) for k in range(STEPS)]

    def absorb(ref, base, k):
        for yy in range(2):
            for b in range(N_TM):
                high, low = split(ref[k, b, :, yy].reshape(GOALS, 128))
                sh[b, pl.ds(k * GOALS, GOALS), pl.ds(base + yy * 128, 128)] = high
                sl[b, pl.ds(k * GOALS, GOALS), pl.ds(base + yy * 128, 128)] = low

    def share(k):
        spread[k].wait()
        return links.group([(own.at[k], other.at[k], partner)], other.at[k], share_sem)

    shared = {}
    for k in range(STEPS):
        for c in range(CHUNKS):
            halos[k, c].wait()
            for y in range(8):
                here = field[k, c, y]
                total = halo[k, c, 0, y] * has_left + halo[k, c, 1, y] * has_right
                if y > 0:
                    total = total + field[k, c, y - 1]
                if y < 7:
                    total = total + field[k, c, y + 1]
                total = total + pltpu.roll(here, 1, 1) * inner_lo + pltpu.roll(here, 127, 1) * inner_hi
                kappa = cond_ref[pl.ds(y, 1), :]
                field[k + 1, c, y] = mask * (here + kappa * (total - 6.0 * here)) + goal[c, y]
            if k + 1 < STEPS:
                halos[k + 1, c] = send_halo(k + 1, c)
            for d in (2, 1, 3):
                links.copy(field.at[k + 1, c, pl.ds(2 * y_peer(d), 2)], own.at[k, t, c], at_y(d), spread_sem, spread[k])
            own[k, t, c] = field[k + 1, c, pl.ds(2 * t, 2)]
        if k > 0:
            shared[k - 1] = share(k - 1)
            absorb(own, 0, k - 1)
        if k > 1:
            shared[k - 2].wait()
            absorb(other, 256, k - 2)
    shared[STEPS - 1] = share(STEPS - 1)
    shared[STEPS - 2].wait()
    absorb(other, 256, STEPS - 2)
    absorb(own, 0, STEPS - 1)
    shared[STEPS - 1].wait()
    absorb(other, 256, STEPS - 1)

    lower, upper = 2 * core, 2 * core + 1

    def gram(i, j):
        return dot3(sh[i], sl[i], sh[j], sl[j], NT)

    for n, (i, j) in enumerate(((lower, lower), (lower, upper), (upper, upper))):
        g = gram(i, j)
        pg[pl.ds(n * 512, 256)] = g[:, :128]
        pg[pl.ds(n * 512 + 256, 256)] = g[:, 128:]
    for n, j in enumerate((2, 3)):
        g = gram(core, j)
        pc[pl.ds(n * 512, 256)] = g[:, :128]
        pc[pl.ds(n * 512 + 256, 256)] = g[:, 128:]

    def offsets(count):
        return sorted(range(1, count), key=lambda d: -min(d, count - d))

    def scatter(src, base, land, length, peer, at, count):
        return links.group([(src.at[rows(base + peer(d) * length, length)], land.at[d - 1], at(d))
                            for d in offsets(count)], land)

    def reduced(src, base, land, length, arrival, place):
        total = src[rows(base + place * length, length)]
        arrival.wait()
        for d in range(land.shape[0]):
            total = total + land[d]
        return total

    def gather(src, dst, base, length, place, at, count):
        return links.group([(src, dst.at[rows(base + place * length, length)], at(d)) for d in offsets(count)],
                           dst.at[pl.ds(base, (count - 1) * length)])

    def stage1(src, landx, landy):
        half = src.shape[0] // 2
        return (scatter(src, 0, landx, half // 4, x_peer, at_x, NX_CHIPS),
                scatter(src, half, landy, half // 4, y_peer, at_y, N_TM))

    def stage2(src, landx, landy, copies, qx, qy, landx2, landy2):
        half = src.shape[0] // 2
        qx[...] = reduced(src, 0, landx, half // 4, copies[0], cx)
        first = scatter(qx, 0, landx2, half // 16, y_peer, at_y, N_TM)
        qy[...] = reduced(src, half, landy, half // 4, copies[1], t)
        return first, scatter(qy, 0, landy2, half // 16, x_peer, at_x, NX_CHIPS)

    def stage3(qx, qy, landx2, landy2, copies, q, land):
        length = qx.shape[0] // 4
        q[pl.ds(0, length)] = reduced(qx, 0, landx2, length, copies[0], t)
        q[pl.ds(length, length)] = reduced(qy, 0, landy2, length, copies[1], cx)
        if q.shape[0] > 2 * length:
            q[pl.ds(2 * length, q.shape[0] - 2 * length)] = jnp.zeros((q.shape[0] - 2 * length, 128), F32)
        return scatter(q, 0, land, q.shape[0] // n_z, z_peer, at_z, n_z)

    def back1(q, land, copies, full):
        length = q.shape[0] // n_z
        full[rows(cz * length, length)] = reduced(q, 0, land, length, copies, cz)
        return gather(full.at[rows(cz * length, length)], full, 0, length, cz, at_z, n_z)

    def back2(full, copies, qx, qy):
        copies.wait()
        length = qx.shape[0] // 4
        first = gather(full.at[pl.ds(0, length)], qx, 0, length, t, at_y, N_TM)
        second = gather(full.at[pl.ds(length, length)], qy, 0, length, cx, at_x, NX_CHIPS)
        qx[rows(t * length, length)] = full[pl.ds(0, length)]
        qy[rows(cx * length, length)] = full[pl.ds(length, length)]
        return first, second

    def back3(qx, qy, copies, dst):
        length = qx.shape[0]
        copies[0].wait()
        first = gather(qx, dst, 0, length, cx, at_x, NX_CHIPS)
        copies[1].wait()
        second = gather(qy, dst, 4 * length, length, t, at_y, N_TM)
        dst[rows(cx * length, length)] = qx[...]
        dst[rows(4 * length + t * length, length)] = qy[...]
        return first, second

    cmat = cb.at[core]
    g1 = stage1(pg, rx1, ry1)
    c1 = stage1(pc, cx1, cy1)
    g2c = stage2(pg, rx1, ry1, g1, qx1, qy1, rx2, ry2)
    c2 = stage2(pc, cx1, cy1, c1, dx1, dy1, cx2, cy2)
    g3 = stage3(qx1, qy1, rx2, ry2, g2c, qz, rz)
    c3 = stage3(dx1, dy1, cx2, cy2, c2, ez, crz)
    g4 = back1(qz, rz, g3, fz)
    c4 = back1(ez, crz, c3, cfz)
    g5 = back2(fz, g4, q2x, q2y)
    c5 = back2(cfz, c4, d2x, d2y)
    g6 = back3(q2x, q2y, g5, gf)
    c6 = back3(d2x, d2y, c5, cmat)
    for arrival in g6:
        arrival.wait()

    def eye(size):
        return (lax.broadcasted_iota(jnp.int32, (size, size), 0)
                == lax.broadcasted_iota(jnp.int32, (size, size), 1)).astype(F32)

    def block(ref, n):
        return jnp.concatenate([ref[pl.ds(n * 512, 256)], ref[pl.ds(n * 512 + 256, 256)]], 1)

    upper_right = block(gf, 1)
    gmat[pl.ds(0, 256), pl.ds(0, 256)] = block(gf, 0)
    gmat[pl.ds(0, 256), pl.ds(256, 256)] = upper_right
    gmat[pl.ds(256, 256), pl.ds(0, 256)] = upper_right.T
    gmat[pl.ds(256, 256), pl.ds(256, 256)] = block(gf, 2)

    def weights(between):
        identity = eye(256)
        trace = jnp.sum(gmat[pl.ds(0, 256), pl.ds(0, 256)] * identity) + jnp.sum(
            gmat[pl.ds(256, 256), pl.ds(256, 256)] * identity)
        energy = trace / 512.0 + 1e-6
        inverse = 1.0 / energy
        norm2 = jnp.float32(0.0)
        for i in range(2):
            for j in range(2):
                part_ = gmat[pl.ds(256 * i, 256), pl.ds(256 * j, 256)] * inverse
                if i == j:
                    part_ = part_ - identity
                s0f[pl.ds(256 * i, 256), pl.ds(256 * j, 256)] = part_
                norm2 = norm2 + jnp.sum(part_ * part_)
        norm = jnp.sqrt(norm2 + 1e-6)
        scale = 1.0 / norm
        for i in range(2):
            r = pl.ds(256 * i, 256)
            value = s0f[r] * scale
            s0f[r] = value
            s0h[r], s0l[r] = split(value)
        between(0)
        for i in range(2):
            r = pl.ds(256 * i, 256)
            zh[r], zl[r] = split(dot3(s0h[r], s0l[r], s0h[...], s0l[...]))
        between(1)
        for i in range(2):
            r = pl.ds(256 * i, 256)
            s1 = 1.5 * s0f[r] - 0.5 * dot3(s0h[r], s0l[r], zh[...], zl[...])
            s1h[r], s1l[r] = split(s1)
            f = s1[:, :256] + s1[:, 256:]
            ff[r] = f
            fh[r], fl[r] = split(f)
        between(2)
        for i in range(2):
            r = pl.ds(256 * i, 256)
            th[r], tl[r] = split(dot3(s1h[r], s1l[r], fh[...], fl[...]))
        for i in range(2):
            r = pl.ds(256 * i, 256)
            u = dot3(s1h[r], s1l[r], th[...], tl[...])
            w = (identity + 1.5 * ff[r] - 0.5 * u) * (0.5 / 2.0 ** 0.5)
            wf[r] = w
            wh[r], wl[r] = split(w)
        between(3)
        kept = jnp.float32(0.0)
        for i in range(2):
            r = pl.ds(256 * i, 256)
            gw = wf[r] + norm * dot3(s0h[r], s0l[r], wh[...], wl[...])
            ff[r] = gw
            kept = kept + jnp.sum(wf[r] * gw)
        return energy, jnp.sqrt(256.0 * energy / (energy * kept + 1e-6))

    state = {}

    def between(n):
        if n == 1:
            for arrival in c6:
                arrival.wait()
            state["c7"] = links.group([(cmat, cmat, partner)], cmat)

    energy, alpha = weights(between)
    for i in range(2):
        wf[pl.ds(256 * i, 256)] = wf[pl.ds(256 * i, 256)] * alpha
    wb[core] = wf[...]
    send_w = links.group([(wb.at[core], wb.at[core], partner)], wb.at[core])
    for i in range(2):
        fh[pl.ds(256 * i, 256)], fl[pl.ds(256 * i, 256)] = split(ff[pl.ds(256 * i, 256)])
    wt[...] = wf[...].T
    ah, al = split(wt[...])
    hb[core] = (energy * alpha) * dot3(ah, al, fh[...], fl[...])
    send_h = links.group([(hb.at[core], hb.at[core], partner)], hb.at[core])
    state["c7"].wait()
    send_w.wait()

    w1h, w1l = split(wb[1])
    th[...] = w1h
    tl[...] = w1l
    for i in range(2):
        r = pl.ds(256 * i, 256)
        ch, cl = split(jnp.concatenate([cb[i, pl.ds(256 * j, 256)] for j in range(4)], 1))
        fh[r], fl[r] = split(dot3(ch, cl, th[...], tl[...]))
    for p in range(2):
        ah, al = split(wb[p].T)
        if p == 0:
            cross = dot3(ah, al, fh[...], fl[...])
            gmat[pl.ds(0, 256), pl.ds(256, 256)] = cross
            gmat[pl.ds(256, 256), pl.ds(0, 256)] = cross.T
        for i in range(2):
            block_h = sh[2 * p + i, :, pl.ds(0, 256)]
            block_l = sl[2 * p + i, :, pl.ds(0, 256)]
            term = dot3(ah[:, 256 * i:256 * i + 256], al[:, 256 * i:256 * i + 256], block_h, block_l)
            merged = term if i == 0 else merged + term
        mh[pl.ds(256 * p, 256)], ml[pl.ds(256 * p, 256)] = split(merged)
    send_h.wait()
    gmat[pl.ds(0, 256), pl.ds(0, 256)] = hb[0]
    gmat[pl.ds(256, 256), pl.ds(256, 256)] = hb[1]
    _, alpha = weights(lambda n: None)
    ah, al = split(wf[...].T)
    bs[...] = alpha * dot3(ah, al, mh[...], ml[...])
    columns = pl.ds(pl.multiple_of(t * 256, 256), 256)
    final = links.group([(bs.at[rows(y_peer(d) * 64, 64)], out_ref.at[:, columns], at_y(d)) for d in (2, 1, 3)],
                        out_ref.at[:, pl.ds(0, 768)])
    out_ref[:, columns] = bs[rows(t * 64, 64)]
    final.wait()
    links.finish()


def shards(terminal, goal_weight, conduct, active_count):
    n_space = lax.axis_size("space")
    n_z = n_space // (2 * NX_CHIPS)

    size = GOALS // CHUNKS

    def f(*shape):
        return pltpu.VMEM(shape, F32)

    def h(*shape):
        return pltpu.VMEM(shape, BF16)

    scratch = [
        f(GOALS * 8, 128), f(GOALS * 8, 128), pltpu.SemaphoreType.DMA((2,)),
        f(STEPS + 1, CHUNKS, 8, size, 128), f(CHUNKS, 8, size, 128),
        f(STEPS, CHUNKS, 2, 8, size, 128),
        f(STEPS, N_TM, CHUNKS, 2, size, 128), f(STEPS, N_TM, CHUNKS, 2, size, 128), h(4, 256, 512), h(4, 256, 512),
        f(1536, 128), f(1024, 128),
        f(3, 192, 128), f(3, 192, 128), f(192, 128), f(192, 128), f(3, 48, 128), f(3, 48, 128),
        f(128, 128), f(n_z - 1, 128 // n_z, 128), f(128, 128), f(192, 128), f(192, 128), f(1536, 128),
        f(3, 128, 128), f(3, 128, 128), f(128, 128), f(128, 128), f(3, 32, 128), f(3, 32, 128),
        f(64, 128), f(n_z - 1, 64 // n_z, 128), f(64, 128), f(128, 128), f(128, 128), f(2, 1024, 128),
        f(512, 512), f(512, 512), h(512, 512), h(512, 512), h(512, 512), h(512, 512), h(512, 512), h(512, 512),
        f(512, 256), h(512, 256), h(512, 256), h(512, 256), h(512, 256), f(512, 256), h(512, 256), h(512, 256),
        f(256, 512), f(2, 512, 256), f(2, 256, 256), h(512, 256), h(512, 256), f(256, 256),
        pltpu.SemaphoreType.DMA((28,)), pltpu.SemaphoreType.DMA((50,)),
    ]
    vmem = pl.BlockSpec(memory_space=pltpu.VMEM)
    place = pl.BlockSpec(memory_space=pl.ANY)

    def body(*refs):
        kernel(n_space, *refs)

    return pl.pallas_call(
        body,
        out_shape=jax.ShapeDtypeStruct((256 // N_TM, 1024), F32),
        in_specs=[place, place, vmem, pl.BlockSpec(memory_space=pltpu.SMEM)],
        out_specs=vmem,
        scratch_shapes=scratch,
        compiler_params=pltpu.CompilerParams(
            collective_id=0, has_side_effects=True, vmem_limit_bytes=56 * 1024 * 1024),
        name="merge_tree",
    )(terminal.reshape(GOALS * 8, 128), goal_weight.reshape(GOALS * 8, 128), conduct.reshape(8, 128), active_count)


def solution(mesh):
    placed = (
        P("tm", None, "space", None, None),
        P(None, "space", None, None),
        P("space", None, None),
        P("tm"),
    )
    return jax.shard_map(
        shards, mesh=mesh, in_specs=placed, out_specs=P("tm", "space"), check_vma=False
    )
```

```python
import jax
import jax.numpy as jnp
from jax import lax
from jax.experimental import pallas as pl
from jax.experimental.pallas import tpu as pltpu
from jax.sharding import PartitionSpec as P

STEPS = 4
GOALS = 64
LAYERS = 8
NX_CHIPS = 4
N_TM = 4
CHUNKS = 8
GROUPS = 4
F32 = jnp.float32
BF16 = jnp.bfloat16


def split(x):
    high = x.astype(BF16)
    return high, (x - high.astype(F32)).astype(BF16)


def dot(a, b, dims):
    return lax.dot_general(a, b, (dims, ((), ())), preferred_element_type=F32)


def dot3(ah, al, bh, bl, dims=((1,), (0,))):
    return dot(ah, bh, dims) + (dot(ah, bl, dims) + dot(al, bh, dims))


NT = ((1,), (1,))


class Arrival:
    def __init__(self, sem, whole):
        self.sem, self.whole, self.done = sem, whole, False

    def wait(self):
        self.done = True
        pltpu.make_async_copy(self.whole, self.whole, self.sem).wait()


class Links:
    def __init__(self, send_sems, recv_sems):
        self.send_sems, self.recv_sems, self.sent, self.arrivals = send_sems, recv_sems, [], []

    def sending(self, whole):
        sem = self.send_sems.at[len(self.sent)]
        self.sent.append(Arrival(sem, whole))
        return sem

    def arrival(self, whole):
        arrival = Arrival(self.recv_sems.at[len(self.arrivals)], whole)
        self.arrivals.append(arrival)
        return arrival

    def group(self, copies, whole, send_sem=None):
        if send_sem is None:
            send_sem = self.sending(whole)
        arrival = self.arrival(whole)
        for src, dst, device in copies:
            self.copy(src, dst, device, send_sem, arrival)
        return arrival

    def copy(self, src, dst, device, send_sem, arrival):
        pltpu.make_async_remote_copy(
            src_ref=src, dst_ref=dst, send_sem=send_sem, recv_sem=arrival.sem,
            device_id=device, device_id_type=pl.DeviceIdType.MESH).start()

    def finish(self):
        for sent in self.sent:
            sent.wait()


def rows(start, size):
    return pl.ds(pl.multiple_of(start, 8), size)


def kernel(n_space, term_ref, goal_ref, cond_ref, count_ref, out_ref,
           term_raw, goal_raw, in_sems, field, goal, halo, own, other, sh, sl,
           pe, pg, pc, ee, ge, cb, *rest):
    early_bufs, pair_bufs, cross_bufs = rest[:10], rest[10:20], rest[20:30]
    (s0f, s0h, s0l, zh, zl, s1h, s1l, ff, fh, fl, th, tl, wf, wh, wl,
           wb, hb, mh, ml, ph, pw, bs, land, send_sems, recv_sems) = rest[30:]
    s = lax.axis_index("space")
    t = lax.axis_index("tm")
    core = s % 2
    chip = s // 2
    cx = chip % NX_CHIPS
    cz = chip // NX_CHIPS
    n_z = n_space // (2 * NX_CHIPS)
    left = (lax.rem(s + n_space - 1, n_space), t)
    right = (lax.rem(s + 1, n_space), t)
    partner = (s + 1 - 2 * core, t)

    def y_peer(d):
        return lax.rem(t + d, N_TM)

    def x_peer(d):
        return lax.rem(cx + d, NX_CHIPS)

    def z_peer(d):
        return lax.rem(cz + d, n_z)

    def at_y(d):
        return (s, y_peer(d))

    def at_x(d):
        return ((cz * NX_CHIPS + x_peer(d)) * 2 + core, t)

    def at_z(d):
        return ((z_peer(d) * NX_CHIPS + cx) * 2 + core, t)

    peers = [left, right] + [at_y(d) for d in range(1, N_TM)] + [at_x(d) for d in range(1, NX_CHIPS)]
    peers += [at_z(d) for d in range(1, n_z)]
    barrier = pltpu.get_barrier_semaphore()
    for peer in peers:
        pl.semaphore_signal(barrier, inc=1, device_id=peer, device_id_type=pl.DeviceIdType.MESH)

    size = GOALS // CHUNKS
    loads = [pltpu.make_async_copy(term_ref, term_raw, in_sems.at[0]),
             pltpu.make_async_copy(goal_ref, goal_raw, in_sems.at[1])]
    for load in loads:
        load.start()
    lane = lax.broadcasted_iota(jnp.int32, (1, 128), 1)
    mask = (lane // (128 // LAYERS) < count_ref[0]).astype(F32)
    loads[0].wait()
    for y in range(8):
        for c in range(CHUNKS):
            field[0, c, y] = term_raw[pl.ds(c * size * 8 + y, size, stride=8), :] * mask
    pl.semaphore_wait(barrier, len(peers))

    links = Links(send_sems, recv_sems)

    halo_sem = links.sending(halo)
    spread_sem = links.sending(own.at[:, pl.ds(0, N_TM - 1)])
    share_sem = links.sending(own)

    def send_halo(k, c):
        return links.group([(field.at[k, c], halo.at[k, c, 0], right), (field.at[k, c], halo.at[k, c, 1], left)],
                           halo.at[k, c], halo_sem)

    def offsets(count):
        return sorted(range(1, count), key=lambda d: -min(d, count - d))

    def scatter(src, base, land, length, peer, at, count):
        return links.group([(src.at[rows(base + peer(d) * length, length)], land.at[d - 1], at(d))
                            for d in offsets(count)], land)

    def reduced(src, base, land, length, arrival, place):
        total = src[rows(base + place * length, length)]
        arrival.wait()
        for d in range(land.shape[0]):
            total = total + land[d]
        return total

    def gather(src, dst, base, length, place, at, count):
        return links.group([(src, dst.at[rows(base + place * length, length)], at(d)) for d in offsets(count)],
                           dst.at[pl.ds(base, (count - 1) * length)])

    def stage1(src, bufs):
        landx, landy = bufs[:2]
        half = src.shape[0] // 2
        return (scatter(src, 0, landx, half // 4, x_peer, at_x, NX_CHIPS),
                scatter(src, half, landy, half // 4, y_peer, at_y, N_TM))

    def stage2(src, bufs, copies):
        landx, landy, qx, qy, landx2, landy2 = bufs[:6]
        half = src.shape[0] // 2
        qx[...] = reduced(src, 0, landx, half // 4, copies[0], cx)
        first = scatter(qx, 0, landx2, half // 16, y_peer, at_y, N_TM)
        qy[...] = reduced(src, half, landy, half // 4, copies[1], t)
        return first, scatter(qy, 0, landy2, half // 16, x_peer, at_x, NX_CHIPS)

    def stage3(bufs, copies):
        qx, qy, landx2, landy2, q, land = bufs[2:8]
        length = qx.shape[0] // 4
        q[pl.ds(0, length)] = reduced(qx, 0, landx2, length, copies[0], t)
        q[pl.ds(length, length)] = reduced(qy, 0, landy2, length, copies[1], cx)
        if q.shape[0] > 2 * length:
            q[pl.ds(2 * length, q.shape[0] - 2 * length)] = jnp.zeros((q.shape[0] - 2 * length, 128), F32)
        return scatter(q, 0, land, q.shape[0] // n_z, z_peer, at_z, n_z)

    def back1(bufs, copies):
        q, land, full = bufs[6:9]
        length = q.shape[0] // n_z
        full[rows(cz * length, length)] = reduced(q, 0, land, length, copies, cz)
        return gather(full.at[rows(cz * length, length)], full, 0, length, cz, at_z, n_z)

    def back2(bufs, copies):
        full = bufs[8]
        qx, qy = bufs[9].at[0], bufs[9].at[1]
        copies.wait()
        length = qx.shape[0] // 4
        first = gather(full.at[pl.ds(0, length)], qx, 0, length, t, at_y, N_TM)
        second = gather(full.at[pl.ds(length, length)], qy, 0, length, cx, at_x, NX_CHIPS)
        qx[rows(t * length, length)] = full[pl.ds(0, length)]
        qy[rows(cx * length, length)] = full[pl.ds(length, length)]
        return first, second

    def back3(bufs, copies, dst):
        qx, qy = bufs[9].at[0], bufs[9].at[1]
        length = qx.shape[0]
        copies[0].wait()
        first = gather(qx, dst, 0, length, cx, at_x, NX_CHIPS)
        copies[1].wait()
        second = gather(qy, dst, 4 * length, length, t, at_y, N_TM)
        dst[rows(cx * length, length)] = qx[...]
        dst[rows(4 * length + t * length, length)] = qy[...]
        return first, second

    has_left = jnp.where(s > 0, 1.0, 0.0).astype(F32)
    has_right = jnp.where(s < n_space - 1, 1.0, 0.0).astype(F32)
    inner_lo = (lane > 0).astype(F32)
    inner_hi = (lane < 127).astype(F32)
    halos = {(0, c): send_halo(0, c) for c in range(CHUNKS)}
    loads[1].wait()
    for y in range(8):
        for c in range(CHUNKS):
            goal[c, y] = goal_raw[pl.ds(c * size * 8 + y, size, stride=8), :] * mask
    final_step, each = STEPS - 1, CHUNKS // GROUPS
    spread = [links.arrival(own.at[k, pl.ds(0, N_TM - 1)]) for k in range(final_step)]
    last_spread = [links.arrival(own.at[final_step, pl.ds(0, N_TM - 1), pl.ds(g * each, each)])
                   for g in range(GROUPS)]

    def absorb(ref, base, k, c, count):
        for yy in range(2):
            for b in range(N_TM):
                high, low = split(ref[k, b, pl.ds(c, count), yy].reshape(count * size, 128))
                place = pl.ds(k * GOALS + c * size, count * size)
                sh[b, place, pl.ds(base + yy * 128, 128)] = high
                sl[b, place, pl.ds(base + yy * 128, 128)] = low

    def share(arrival, k, c, count):
        arrival.wait()
        some = (k, slice(None), pl.ds(c, count))
        return links.group([(own.at[some], other.at[some], partner)], other.at[some], share_sem)

    shared = {}
    for k in range(STEPS):
        for c in range(CHUNKS):
            halos[k, c].wait()
            for y in range(8):
                here = field[k, c, y]
                total = halo[k, c, 0, y] * has_left + halo[k, c, 1, y] * has_right
                if y > 0:
                    total = total + field[k, c, y - 1]
                if y < 7:
                    total = total + field[k, c, y + 1]
                total = total + pltpu.roll(here, 1, 1) * inner_lo + pltpu.roll(here, 127, 1) * inner_hi
                kappa = cond_ref[pl.ds(y, 1), :]
                field[k + 1, c, y] = mask * (here + kappa * (total - 6.0 * here)) + goal[c, y]
            if k + 1 < STEPS:
                halos[k + 1, c] = send_halo(k + 1, c)
            for d in (2, 1, 3):
                links.copy(field.at[k + 1, c, pl.ds(2 * y_peer(d), 2)], own.at[k, t, c], at_y(d), spread_sem,
                           spread[k] if k < final_step else last_spread[c // each])
            own[k, t, c] = field[k + 1, c, pl.ds(2 * t, 2)]
        if k > 0:
            shared[k - 1] = share(spread[k - 1], k - 1, 0, CHUNKS)
            absorb(own, 0, k - 1, 0, CHUNKS)
        if k > 1:
            shared[k - 2].wait()
            absorb(other, 256, k - 2, 0, CHUNKS)
    shared[final_step - 1].wait()
    absorb(other, 256, final_step - 1, 0, CHUNKS)

    lower, upper = 2 * core, 2 * core + 1
    first, second = pl.ds(0, 128), pl.ds(128, 128)

    def both(ref, i, j):
        return jnp.concatenate([ref[i, first], ref[j, first]], 0)

    def early(i, j, k):
        return dot3(sh[i, first], sl[i, first], both(sh, j, k), both(sl, j, k), NT)

    g = early(lower, lower, upper)
    pe[pl.ds(0, 128)] = g[:, :128]
    pe[pl.ds(128, 128)] = g[:, 128:]
    g = dot3(sh[upper, first], sl[upper, first], sh[upper, first], sl[upper, first], NT)
    pe[pl.ds(256, 128)] = g
    g = early(core, 2, 3)
    pe[pl.ds(384, 128)] = g[:, :128]
    pg[pl.ds(896, 128)] = g[:, 128:]
    e1 = stage1(pe, early_bufs)
    last_shared = []
    for g in range(GROUPS):
        last_shared.append(share(last_spread[g], final_step, g * each, each))
        absorb(own, 0, final_step, g * each, each)
    for g in range(GROUPS):
        last_shared[g].wait()
        absorb(other, 256, final_step, g * each, each)

    e2 = stage2(pe, early_bufs, e1)

    def put(ref, n, value):
        ref[pl.ds(128 * n, 128)] = value

    def late(n, i):
        g = dot3(sh[i, second], sl[i, second], sh[i], sl[i], NT)
        put(pg, n, g[:, :128])
        put(pg, n + 1, g[:, 128:])

    def mixed(ref, n, i, j):
        g = dot3(sh[i], sl[i], sh[j], sl[j], NT)
        put(ref, n, g[:128, 128:])
        put(ref, n + 1, g[128:, :128])
        put(ref, n + 2, g[128:, 128:])

    late(0, lower)
    mixed(pg, 2, lower, upper)
    late(5, upper)
    g1 = stage1(pg, pair_bufs)
    mixed(pc, 0, core, 2)
    mixed(pc, 3, core, 3)

    cmat = cb.at[core, pl.ds(0, 768)]
    c1 = stage1(pc, cross_bufs)
    e3 = stage3(early_bufs, e2)
    g2 = stage2(pg, pair_bufs, g1)
    c2 = stage2(pc, cross_bufs, c1)
    e4 = back1(early_bufs, e3)
    g3 = stage3(pair_bufs, g2)
    c3 = stage3(cross_bufs, c2)
    e5 = back2(early_bufs, e4)
    g4 = back1(pair_bufs, g3)
    c4 = back1(cross_bufs, c3)
    e6 = back3(early_bufs, e5, ee)
    g5 = back2(pair_bufs, g4)
    c5 = back2(cross_bufs, c4)
    g6 = back3(pair_bufs, g5, ge)
    c6 = back3(cross_bufs, c5, cmat)
    for arrival in e6:
        arrival.wait()
    for arrival in g6:
        arrival.wait()

    identity = (lax.broadcasted_iota(jnp.int32, (256, 256), 0)
                == lax.broadcasted_iota(jnp.int32, (256, 256), 1)).astype(F32)
    halves = (pl.ds(0, 256), pl.ds(256, 256))

    def square(upper_left, lower_left, lower_right):
        top = jnp.concatenate([upper_left, lower_left.T], 1)
        return jnp.concatenate([top, jnp.concatenate([lower_left, lower_right], 1)], 0)

    def tile(ref, n):
        return ref[pl.ds(128 * n, 128)]

    def put_s0(i, j, value):
        s0f[halves[i], halves[j]] = value
        s0h[halves[i], halves[j]], s0l[halves[i], halves[j]] = split(value)

    def weights(g00, g01, g11):
        energy = jnp.sum((g00 + g11) * identity) / 512.0 + 1e-6
        inverse = 1.0 / energy
        upper, lower_, across = g00 * inverse - identity, g11 * inverse - identity, g01 * inverse
        put_s0(0, 0, upper)
        put_s0(1, 1, lower_)
        put_s0(0, 1, across)
        put_s0(1, 0, across.T)
        norm2 = jnp.sum(upper * upper + lower_ * lower_ + 2.0 * (across * across)) + 1e-6
        scale = 1.0 / jnp.sqrt(norm2)
        for r in halves:
            zh[r], zl[r] = split(dot3(s0h[r], s0l[r], s0h[...], s0l[...]))
        folded = None
        for r in halves:
            s1 = (1.5 * scale) * s0f[r] - (0.5 * scale / norm2) * dot3(s0h[r], s0l[r], zh[...], zl[...])
            s1h[r], s1l[r] = split(s1)
            folded = s1 if folded is None else folded + s1
        ff[...] = folded
        fh[...], fl[...] = split(folded)
        th[...], tl[...] = split(dot3(fh[...], fl[...], s1h[...], s1l[...]))
        u = dot3(th[...], tl[...], s1h[...], s1l[...])
        w = (jnp.concatenate([identity, identity], 1) + 1.5 * ff[...] - 0.5 * u) * (0.5 / 2.0 ** 0.5)
        wf[...] = w
        wh[...], wl[...] = split(w)
        return energy

    def kept_part(energy):
        gw = wf[...] + dot3(wh[...], wl[...], s0h[...], s0l[...])
        ff[...] = gw
        kept = energy * jnp.sum(wf[...] * gw)
        return jnp.sqrt(energy * 256.0 / (kept + 1e-6))

    energy = weights(
        square(tile(ee, 0), tile(ge, 0), tile(ge, 1)),
        jnp.concatenate([jnp.concatenate([tile(ee, 1), tile(ge, 2)], 1),
                         jnp.concatenate([tile(ge, 3), tile(ge, 4)], 1)], 0),
        square(tile(ee, 2), tile(ge, 5), tile(ge, 6)))
    wb[core] = wf[...]
    send_w = links.group([(wb.at[core], wb.at[core], partner)], wb.at[core])
    for arrival in c6:
        arrival.wait()
    cb[core, pl.ds(768, 128)] = tile(ee, 3)
    cb[core, pl.ds(896, 128)] = tile(ge, 7)
    send_c = links.group([(cb.at[core], cb.at[core], partner)], cb.at[core])
    alpha = kept_part(energy)
    fh[...], fl[...] = split(ff[...])
    hb[core, pl.ds(0, 256)] = (energy * alpha * alpha) * dot3(fh[...], fl[...], wh[...], wl[...], NT)
    hb[core, pl.ds(256, 8)] = jnp.full((8, 256), alpha, F32)
    send_h = links.group([(hb.at[core], hb.at[core], partner)], hb.at[core])
    send_w.wait()

    merged = []
    for p in range(2):
        wh[...], wl[...] = split(wb[p])
        terms = [dot3(wh[:, 256 * i:256 * i + 256], wl[:, 256 * i:256 * i + 256],
                      sh[2 * p + i, :, pl.ds(0, 256)], sl[2 * p + i, :, pl.ds(0, 256)]) for i in range(2)]
        merged.append(terms[0] + terms[1])
    send_c.wait()
    for i in range(2):
        c_rows = jnp.concatenate([jnp.concatenate([cb[i, pl.ds(128 * n, 128)] for n in order], 1)
                                  for order in ((6, 0, 7, 3), (1, 2, 4, 5))], 0)
        ch, cl = split(c_rows)
        ph[halves[i]], pw[halves[i]] = split(dot3(ch, cl, wh[...], wl[...], NT))
    wh[...], wl[...] = split(wb[0])
    cross = dot3(wh[...], wl[...], ph[...], pw[...])
    send_h.wait()
    alphas = [hb[p, pl.ds(256, 1)] for p in range(2)]
    for p in range(2):
        mh[halves[p]], ml[halves[p]] = split(merged[p] * alphas[p])
    energy = weights(hb[0, pl.ds(0, 256)], cross * (alphas[0] * alphas[1]), hb[1, pl.ds(0, 256)])
    bs[...] = dot3(wh[...], wl[...], mh[...], ml[...])
    columns = pl.ds(pl.multiple_of(t * 256, 256), 256)
    final = links.group([(bs.at[rows(y_peer(d) * 64, 64)], land.at[:, columns], at_y(d)) for d in (2, 1, 3)],
                        land.at[:, pl.ds(0, 768)])
    land[:, columns] = bs[rows(t * 64, 64)]
    alpha = kept_part(energy)
    final.wait()
    out_ref[...] = alpha * land[...]
    links.finish()


def shards(terminal, goal_weight, conduct, active_count):
    n_space = lax.axis_size("space")
    n_z = n_space // (2 * NX_CHIPS)

    size = GOALS // CHUNKS

    def f(*shape):
        return pltpu.VMEM(shape, F32)

    def h(*shape):
        return pltpu.VMEM(shape, BF16)

    def stages(length):
        one, two = length // 8, length // 32
        pad = -(-2 * two // (8 * n_z)) * 8 * n_z
        return [f(3, one, 128), f(3, one, 128), f(one, 128), f(one, 128), f(3, two, 128), f(3, two, 128),
                f(pad, 128), f(n_z - 1, pad // n_z, 128), f(pad, 128), f(2, one, 128)]

    scratch = [
        f(GOALS * 8, 128), f(GOALS * 8, 128), pltpu.SemaphoreType.DMA((2,)),
        f(STEPS + 1, CHUNKS, 8, size, 128), f(CHUNKS, 8, size, 128),
        f(STEPS, CHUNKS, 2, 8, size, 128),
        f(STEPS, N_TM, CHUNKS, 2, size, 128), f(STEPS, N_TM, CHUNKS, 2, size, 128), h(4, 256, 512), h(4, 256, 512),
        f(512, 128), f(1024, 128), f(768, 128), f(512, 128), f(1024, 128), f(2, 1024, 128),
        *stages(512), *stages(1024), *stages(768),
        f(512, 512), h(512, 512), h(512, 512), h(512, 512), h(512, 512), h(512, 512), h(512, 512),
        f(256, 512), h(256, 512), h(256, 512), h(256, 512), h(256, 512), f(256, 512), h(256, 512), h(256, 512),
        f(2, 256, 512), f(2, 264, 256), h(512, 256), h(512, 256), h(512, 256), h(512, 256), f(256, 256), f(64, 1024),
        pltpu.SemaphoreType.DMA((37,)), pltpu.SemaphoreType.DMA((80,)),
    ]
    vmem = pl.BlockSpec(memory_space=pltpu.VMEM)
    place = pl.BlockSpec(memory_space=pl.ANY)

    def body(*refs):
        kernel(n_space, *refs)

    return pl.pallas_call(
        body,
        out_shape=jax.ShapeDtypeStruct((256 // N_TM, 1024), F32),
        in_specs=[place, place, vmem, pl.BlockSpec(memory_space=pltpu.SMEM)],
        out_specs=vmem,
        scratch_shapes=scratch,
        compiler_params=pltpu.CompilerParams(
            collective_id=0, has_side_effects=True, vmem_limit_bytes=32 * 1024 * 1024),
        name="merge_tree",
    )(terminal.reshape(GOALS * 8, 128), goal_weight.reshape(GOALS * 8, 128), conduct.reshape(8, 128), active_count)


def solution(mesh):
    placed = (
        P("tm", None, "space", None, None),
        P(None, "space", None, None),
        P("space", None, None),
        P("tm"),
    )
    return jax.shard_map(
        shards, mesh=mesh, in_specs=placed, out_specs=P("tm", "space"), check_vma=False
    )
```

```python
import jax
import jax.numpy as jnp
from jax import lax
from jax.experimental import pallas as pl
from jax.experimental.pallas import tpu as pltpu
from jax.sharding import PartitionSpec as P

STEPS = 4
GOALS = 64
LAYERS = 8
NX_CHIPS = 4
N_TM = 4
CHUNKS = 8
GROUPS = 4
F32 = jnp.float32
BF16 = jnp.bfloat16


def split(x):
    high = x.astype(BF16)
    return high, (x - high.astype(F32)).astype(BF16)


def dot(a, b, dims):
    return lax.dot_general(a, b, (dims, ((), ())), preferred_element_type=F32)


def dot3(ah, al, bh, bl, dims=((1,), (0,))):
    return dot(ah, bh, dims) + (dot(ah, bl, dims) + dot(al, bh, dims))


NT = ((1,), (1,))


class Arrival:
    def __init__(self, sem, whole):
        self.sem, self.whole, self.done = sem, whole, False

    def wait(self):
        self.done = True
        pltpu.make_async_copy(self.whole, self.whole, self.sem).wait()


class Links:
    def __init__(self, send_sems, recv_sems):
        self.send_sems, self.recv_sems, self.sent, self.arrivals = send_sems, recv_sems, [], []

    def sending(self, whole):
        sem = self.send_sems.at[len(self.sent)]
        self.sent.append(Arrival(sem, whole))
        return sem

    def arrival(self, whole):
        arrival = Arrival(self.recv_sems.at[len(self.arrivals)], whole)
        self.arrivals.append(arrival)
        return arrival

    def group(self, copies, whole, send_sem=None):
        if send_sem is None:
            send_sem = self.sending(whole)
        arrival = self.arrival(whole)
        for src, dst, device in copies:
            self.copy(src, dst, device, send_sem, arrival)
        return arrival

    def copy(self, src, dst, device, send_sem, arrival):
        pltpu.make_async_remote_copy(
            src_ref=src, dst_ref=dst, send_sem=send_sem, recv_sem=arrival.sem,
            device_id=device, device_id_type=pl.DeviceIdType.MESH).start()

    def finish(self):
        for sent in self.sent:
            if not sent.done:
                sent.wait()


def rows(start, size):
    return pl.ds(pl.multiple_of(start, 8), size)


def kernel(n_space, term_ref, goal_ref, cond_ref, count_ref, out_ref,
           term_raw, goal_raw, in_sems, field, goal, halo, own, other, sh, sl,
           pe, pg, pc, ee, ge, cb, *rest):
    early_bufs, pair_bufs, cross_bufs = rest[:10], rest[10:20], rest[20:30]
    (s0f, s0h, s0l, zh, zl, s1h, s1l, ff, fh, fl, th, tl, wf, wh, wl,
           wb, hb, mh, ml, ph, pw, bs, land, send_sems, recv_sems) = rest[30:]
    s = lax.axis_index("space")
    t = lax.axis_index("tm")
    core = s % 2
    chip = s // 2
    cx = chip % NX_CHIPS
    cz = chip // NX_CHIPS
    n_z = n_space // (2 * NX_CHIPS)
    left = (lax.rem(s + n_space - 1, n_space), t)
    right = (lax.rem(s + 1, n_space), t)
    partner = (s + 1 - 2 * core, t)

    def y_peer(d):
        return lax.rem(t + d, N_TM)

    def x_peer(d):
        return lax.rem(cx + d, NX_CHIPS)

    def z_peer(d):
        return lax.rem(cz + d, n_z)

    def at_y(d):
        return (s, y_peer(d))

    def at_x(d):
        return ((cz * NX_CHIPS + x_peer(d)) * 2 + core, t)

    def at_z(d):
        return ((z_peer(d) * NX_CHIPS + cx) * 2 + core, t)

    peers = [left, right] + [at_y(d) for d in range(1, N_TM)] + [at_x(d) for d in range(1, NX_CHIPS)]
    peers += [at_z(d) for d in range(1, n_z)]
    barrier = pltpu.get_barrier_semaphore()
    for peer in peers:
        pl.semaphore_signal(barrier, inc=1, device_id=peer, device_id_type=pl.DeviceIdType.MESH)

    size = GOALS // CHUNKS
    loads = [pltpu.make_async_copy(term_ref, term_raw, in_sems.at[0]),
             pltpu.make_async_copy(goal_ref, goal_raw, in_sems.at[1])]
    for load in loads:
        load.start()
    lane = lax.broadcasted_iota(jnp.int32, (1, 128), 1)
    mask = (lane // (128 // LAYERS) < count_ref[0]).astype(F32)
    loads[0].wait()
    for y in range(8):
        for c in range(CHUNKS):
            field[0, c, y] = term_raw[pl.ds(c * size * 8 + y, size, stride=8), :] * mask
    pl.semaphore_wait(barrier, len(peers))

    links = Links(send_sems, recv_sems)

    halo_sem = links.sending(halo)
    spread_sem = links.sending(own.at[:, pl.ds(0, N_TM - 1)])
    share_sem = links.sending(own)

    def send_halo(k, c):
        return links.group([(field.at[k, c], halo.at[k, c, 0], right), (field.at[k, c], halo.at[k, c, 1], left)],
                           halo.at[k, c], halo_sem)

    def offsets(count):
        return sorted(range(1, count), key=lambda d: -min(d, count - d))

    def scatter(src, base, land, length, peer, at, count):
        return links.group([(src.at[rows(base + peer(d) * length, length)], land.at[d - 1], at(d))
                            for d in offsets(count)], land)

    def reduced(src, base, land, length, arrival, place):
        total = src[rows(base + place * length, length)]
        arrival.wait()
        for d in range(land.shape[0]):
            total = total + land[d]
        return total

    def gather(src, dst, base, length, place, at, count):
        return links.group([(src, dst.at[rows(base + place * length, length)], at(d)) for d in offsets(count)],
                           dst.at[pl.ds(base, (count - 1) * length)])

    def stage1(src, bufs):
        landx, landy = bufs[:2]
        half = src.shape[0] // 2
        return (scatter(src, 0, landx, half // 4, x_peer, at_x, NX_CHIPS),
                scatter(src, half, landy, half // 4, y_peer, at_y, N_TM))

    def stage2(src, bufs, copies):
        landx, landy, qx, qy, landx2, landy2 = bufs[:6]
        half = src.shape[0] // 2
        qx[...] = reduced(src, 0, landx, half // 4, copies[0], cx)
        first = scatter(qx, 0, landx2, half // 16, y_peer, at_y, N_TM)
        qy[...] = reduced(src, half, landy, half // 4, copies[1], t)
        return first, scatter(qy, 0, landy2, half // 16, x_peer, at_x, NX_CHIPS)

    def stage3(bufs, copies):
        qx, qy, landx2, landy2, q, land = bufs[2:8]
        length = qx.shape[0] // 4
        q[pl.ds(0, length)] = reduced(qx, 0, landx2, length, copies[0], t)
        q[pl.ds(length, length)] = reduced(qy, 0, landy2, length, copies[1], cx)
        if q.shape[0] > 2 * length:
            q[pl.ds(2 * length, q.shape[0] - 2 * length)] = jnp.zeros((q.shape[0] - 2 * length, 128), F32)
        return scatter(q, 0, land, q.shape[0] // n_z, z_peer, at_z, n_z)

    def back1(bufs, copies):
        q, land, full = bufs[6:9]
        length = q.shape[0] // n_z
        full[rows(cz * length, length)] = reduced(q, 0, land, length, copies, cz)
        return gather(full.at[rows(cz * length, length)], full, 0, length, cz, at_z, n_z)

    def back2(bufs, copies):
        full = bufs[8]
        qx, qy = bufs[9].at[0], bufs[9].at[1]
        copies.wait()
        length = qx.shape[0] // 4
        first = gather(full.at[pl.ds(0, length)], qx, 0, length, t, at_y, N_TM)
        second = gather(full.at[pl.ds(length, length)], qy, 0, length, cx, at_x, NX_CHIPS)
        qx[rows(t * length, length)] = full[pl.ds(0, length)]
        qy[rows(cx * length, length)] = full[pl.ds(length, length)]
        return first, second

    def back3(bufs, copies, dst):
        qx, qy = bufs[9].at[0], bufs[9].at[1]
        length = qx.shape[0]
        copies[0].wait()
        first = gather(qx, dst, 0, length, cx, at_x, NX_CHIPS)
        copies[1].wait()
        second = gather(qy, dst, 4 * length, length, t, at_y, N_TM)
        dst[rows(cx * length, length)] = qx[...]
        dst[rows(4 * length + t * length, length)] = qy[...]
        return first, second

    has_left = jnp.where(s > 0, 1.0, 0.0).astype(F32)
    has_right = jnp.where(s < n_space - 1, 1.0, 0.0).astype(F32)
    inner_lo = (lane > 0).astype(F32)
    inner_hi = (lane < 127).astype(F32)
    halos = {(0, c): send_halo(0, c) for c in range(CHUNKS)}
    loads[1].wait()
    for y in range(8):
        for c in range(CHUNKS):
            goal[c, y] = goal_raw[pl.ds(c * size * 8 + y, size, stride=8), :] * mask
    final_step, each = STEPS - 1, CHUNKS // GROUPS
    spread = [links.arrival(own.at[k, pl.ds(0, N_TM - 1)]) for k in range(final_step)]
    last_spread = [links.arrival(own.at[final_step, pl.ds(0, N_TM - 1), pl.ds(g * each, each)])
                   for g in range(GROUPS)]

    def absorb(ref, base, k, c, count):
        for yy in range(2):
            for b in range(N_TM):
                high, low = split(ref[k, b, pl.ds(c, count), yy].reshape(count * size, 128))
                place = pl.ds(k * GOALS + c * size, count * size)
                sh[b, place, pl.ds(base + yy * 128, 128)] = high
                sl[b, place, pl.ds(base + yy * 128, 128)] = low

    def share(arrival, k, c, count):
        arrival.wait()
        some = (k, slice(None), pl.ds(c, count))
        return links.group([(own.at[some], other.at[some], partner)], other.at[some], share_sem)

    shared = {}
    for k in range(STEPS):
        for c in range(CHUNKS):
            halos[k, c].wait()
            for y in range(8):
                here = field[k, c, y]
                total = halo[k, c, 0, y] * has_left + halo[k, c, 1, y] * has_right
                if y > 0:
                    total = total + field[k, c, y - 1]
                if y < 7:
                    total = total + field[k, c, y + 1]
                total = total + pltpu.roll(here, 1, 1) * inner_lo + pltpu.roll(here, 127, 1) * inner_hi
                kappa = cond_ref[pl.ds(y, 1), :]
                field[k + 1, c, y] = mask * (here + kappa * (total - 6.0 * here)) + goal[c, y]
            if k + 1 < STEPS:
                halos[k + 1, c] = send_halo(k + 1, c)
            for d in (2, 1, 3):
                links.copy(field.at[k + 1, c, pl.ds(2 * y_peer(d), 2)], own.at[k, t, c], at_y(d), spread_sem,
                           spread[k] if k < final_step else last_spread[c // each])
            own[k, t, c] = field[k + 1, c, pl.ds(2 * t, 2)]
        if k > 0:
            shared[k - 1] = share(spread[k - 1], k - 1, 0, CHUNKS)
            absorb(own, 0, k - 1, 0, CHUNKS)
        if k > 1:
            shared[k - 2].wait()
            absorb(other, 256, k - 2, 0, CHUNKS)
    shared[final_step - 1].wait()
    absorb(other, 256, final_step - 1, 0, CHUNKS)

    lower, upper = 2 * core, 2 * core + 1
    first, second = pl.ds(0, 128), pl.ds(128, 128)

    def both(ref, i, j):
        return jnp.concatenate([ref[i, first], ref[j, first]], 0)

    def early(i, j, k):
        return dot3(sh[i, first], sl[i, first], both(sh, j, k), both(sl, j, k), NT)

    g = early(lower, lower, upper)
    pe[pl.ds(0, 128)] = g[:, :128]
    pe[pl.ds(128, 128)] = g[:, 128:]
    g = dot3(sh[upper, first], sl[upper, first], sh[upper, first], sl[upper, first], NT)
    pe[pl.ds(256, 128)] = g
    g = early(core, 2, 3)
    pe[pl.ds(384, 128)] = g[:, :128]
    pg[pl.ds(896, 128)] = g[:, 128:]
    e1 = stage1(pe, early_bufs)
    last_shared = []
    for g in range(GROUPS):
        last_shared.append(share(last_spread[g], final_step, g * each, each))
        absorb(own, 0, final_step, g * each, each)
    for g in range(GROUPS):
        last_shared[g].wait()
        absorb(other, 256, final_step, g * each, each)

    e2 = stage2(pe, early_bufs, e1)

    def put(ref, n, value):
        ref[pl.ds(128 * n, 128)] = value

    def late(n, i):
        g = dot3(sh[i, second], sl[i, second], sh[i], sl[i], NT)
        put(pg, n, g[:, :128])
        put(pg, n + 1, g[:, 128:])

    def mixed(ref, n, i, j):
        g = dot3(sh[i], sl[i], sh[j], sl[j], NT)
        put(ref, n, g[:128, 128:])
        put(ref, n + 1, g[128:, :128])
        put(ref, n + 2, g[128:, 128:])

    late(0, lower)
    mixed(pg, 2, lower, upper)
    late(5, upper)
    g1 = stage1(pg, pair_bufs)
    mixed(pc, 0, core, 2)
    mixed(pc, 3, core, 3)

    cmat = cb.at[core, pl.ds(0, 768)]
    c1 = stage1(pc, cross_bufs)
    e3 = stage3(early_bufs, e2)
    g2 = stage2(pg, pair_bufs, g1)
    c2 = stage2(pc, cross_bufs, c1)
    e4 = back1(early_bufs, e3)
    g3 = stage3(pair_bufs, g2)
    c3 = stage3(cross_bufs, c2)
    e5 = back2(early_bufs, e4)
    g4 = back1(pair_bufs, g3)
    c4 = back1(cross_bufs, c3)
    e6 = back3(early_bufs, e5, ee)
    g5 = back2(pair_bufs, g4)
    c5 = back2(cross_bufs, c4)
    g6 = back3(pair_bufs, g5, ge)
    c6 = back3(cross_bufs, c5, cmat)
    for arrival in e6:
        arrival.wait()
    for arrival in g6:
        arrival.wait()

    identity = (lax.broadcasted_iota(jnp.int32, (256, 256), 0)
                == lax.broadcasted_iota(jnp.int32, (256, 256), 1)).astype(F32)
    halves = (pl.ds(0, 256), pl.ds(256, 256))

    def square(upper_left, lower_left, lower_right):
        top = jnp.concatenate([upper_left, lower_left.T], 1)
        return jnp.concatenate([top, jnp.concatenate([lower_left, lower_right], 1)], 0)

    def tile(ref, n):
        return ref[pl.ds(128 * n, 128)]

    def put_s0(i, j, value):
        s0f[halves[i], halves[j]] = value
        s0h[halves[i], halves[j]], s0l[halves[i], halves[j]] = split(value)

    def weights(g00, g01, g11, trace):
        energy = trace / 512.0 + 1e-6
        inverse = 1.0 / energy
        upper, lower_, across = g00 * inverse - identity, g11 * inverse - identity, g01 * inverse
        put_s0(0, 0, upper)
        put_s0(1, 1, lower_)
        put_s0(0, 1, across)
        put_s0(1, 0, across.T)
        norm2 = jnp.sum(upper * upper + lower_ * lower_ + 2.0 * (across * across)) + 1e-6
        scale = 1.0 / jnp.sqrt(norm2)
        for r in halves:
            zh[r], zl[r] = split(dot3(s0h[r], s0l[r], s0h[...], s0l[...]))
        folded = None
        for r in halves:
            s1 = (1.5 * scale) * s0f[r] - (0.5 * scale / norm2) * dot3(s0h[r], s0l[r], zh[...], zl[...])
            s1h[r], s1l[r] = split(s1)
            folded = s1 if folded is None else folded + s1
        ff[...] = folded
        fh[...], fl[...] = split(folded)
        th[...], tl[...] = split(dot3(fh[...], fl[...], s1h[...], s1l[...]))
        u = dot3(th[...], tl[...], s1h[...], s1l[...])
        w = (jnp.concatenate([identity, identity], 1) + 1.5 * ff[...] - 0.5 * u) * (0.5 / 2.0 ** 0.5)
        wf[...] = w
        wh[...], wl[...] = split(w)
        return energy

    def kept_part(energy):
        gw = wf[...] + dot3(wh[...], wl[...], s0h[...], s0l[...])
        ff[...] = gw
        kept = energy * jnp.sum(wf[...] * gw)
        alpha = jnp.sqrt(energy * 256.0 / (kept + 1e-6))
        return alpha, alpha * alpha * kept

    trace = jnp.sum((tile(ee, 0) + tile(ge, 1) + tile(ee, 2) + tile(ge, 6)) * identity[:128, :128])
    energy = weights(
        square(tile(ee, 0), tile(ge, 0), tile(ge, 1)),
        jnp.concatenate([jnp.concatenate([tile(ee, 1), tile(ge, 2)], 1),
                         jnp.concatenate([tile(ge, 3), tile(ge, 4)], 1)], 0),
        square(tile(ee, 2), tile(ge, 5), tile(ge, 6)), trace)
    wb[core] = wf[...]
    send_w = links.group([(wb.at[core], wb.at[core], partner)], wb.at[core])
    for arrival in c6:
        arrival.wait()
    cb[core, pl.ds(768, 128)] = tile(ee, 3)
    cb[core, pl.ds(896, 128)] = tile(ge, 7)
    send_c = links.group([(cb.at[core], cb.at[core], partner)], cb.at[core])
    alpha, trace = kept_part(energy)
    fh[...], fl[...] = split(ff[...])
    hb[core, pl.ds(0, 256)] = (energy * alpha * alpha) * dot3(fh[...], fl[...], wh[...], wl[...], NT)
    hb[core, pl.ds(256, 8)] = jnp.full((8, 256), alpha, F32)
    hb[core, pl.ds(264, 8)] = jnp.full((8, 256), trace, F32)
    send_h = links.group([(hb.at[core], hb.at[core], partner)], hb.at[core])
    send_w.wait()

    merged = []
    for p in range(2):
        wh[...], wl[...] = split(wb[p])
        terms = [dot3(wh[:, 256 * i:256 * i + 256], wl[:, 256 * i:256 * i + 256],
                      sh[2 * p + i, :, pl.ds(0, 256)], sl[2 * p + i, :, pl.ds(0, 256)]) for i in range(2)]
        merged.append(terms[0] + terms[1])
    send_c.wait()
    for i in range(2):
        c_rows = jnp.concatenate([jnp.concatenate([cb[i, pl.ds(128 * n, 128)] for n in order], 1)
                                  for order in ((6, 0, 7, 3), (1, 2, 4, 5))], 0)
        ch, cl = split(c_rows)
        ph[halves[i]], pw[halves[i]] = split(dot3(ch, cl, wh[...], wl[...], NT))
    wh[...], wl[...] = split(wb[0])
    cross = dot3(wh[...], wl[...], ph[...], pw[...])
    send_h.wait()
    alphas = [hb[p, pl.ds(256, 1)] for p in range(2)]
    for p in range(2):
        mh[halves[p]], ml[halves[p]] = split(merged[p] * alphas[p])
    energy = weights(hb[0, pl.ds(0, 256)], cross * (alphas[0] * alphas[1]), hb[1, pl.ds(0, 256)],
                     jnp.sum(hb[0, pl.ds(264, 1), pl.ds(0, 1)] + hb[1, pl.ds(264, 1), pl.ds(0, 1)]))
    bs[...] = dot3(wh[...], wl[...], mh[...], ml[...])
    columns = pl.ds(pl.multiple_of(t * 256, 256), 256)
    final = links.group([(bs.at[rows(y_peer(d) * 64, 64)], land.at[:, columns], at_y(d)) for d in (2, 1, 3)],
                        land.at[:, pl.ds(0, 768)])
    land[:, columns] = bs[rows(t * 64, 64)]
    alpha = kept_part(energy)[0]
    for sent in links.sent[:-1]:
        sent.wait()
    final.wait()
    out_ref[...] = alpha * land[...]
    links.finish()


def shards(terminal, goal_weight, conduct, active_count):
    n_space = lax.axis_size("space")
    n_z = n_space // (2 * NX_CHIPS)

    size = GOALS // CHUNKS

    def f(*shape):
        return pltpu.VMEM(shape, F32)

    def h(*shape):
        return pltpu.VMEM(shape, BF16)

    def stages(length):
        one, two = length // 8, length // 32
        pad = -(-2 * two // (8 * n_z)) * 8 * n_z
        return [f(3, one, 128), f(3, one, 128), f(one, 128), f(one, 128), f(3, two, 128), f(3, two, 128),
                f(pad, 128), f(n_z - 1, pad // n_z, 128), f(pad, 128), f(2, one, 128)]

    scratch = [
        f(GOALS * 8, 128), f(GOALS * 8, 128), pltpu.SemaphoreType.DMA((2,)),
        f(STEPS + 1, CHUNKS, 8, size, 128), f(CHUNKS, 8, size, 128),
        f(STEPS, CHUNKS, 2, 8, size, 128),
        f(STEPS, N_TM, CHUNKS, 2, size, 128), f(STEPS, N_TM, CHUNKS, 2, size, 128), h(4, 256, 512), h(4, 256, 512),
        f(512, 128), f(1024, 128), f(768, 128), f(512, 128), f(1024, 128), f(2, 1024, 128),
        *stages(512), *stages(1024), *stages(768),
        f(512, 512), h(512, 512), h(512, 512), h(512, 512), h(512, 512), h(512, 512), h(512, 512),
        f(256, 512), h(256, 512), h(256, 512), h(256, 512), h(256, 512), f(256, 512), h(256, 512), h(256, 512),
        f(2, 256, 512), f(2, 272, 256), h(512, 256), h(512, 256), h(512, 256), h(512, 256), f(256, 256), f(64, 1024),
        pltpu.SemaphoreType.DMA((37,)), pltpu.SemaphoreType.DMA((80,)),
    ]
    vmem = pl.BlockSpec(memory_space=pltpu.VMEM)
    place = pl.BlockSpec(memory_space=pl.ANY)

    def body(*refs):
        kernel(n_space, *refs)

    return pl.pallas_call(
        body,
        out_shape=jax.ShapeDtypeStruct((256 // N_TM, 1024), F32),
        in_specs=[place, place, vmem, pl.BlockSpec(memory_space=pltpu.SMEM)],
        out_specs=vmem,
        scratch_shapes=scratch,
        compiler_params=pltpu.CompilerParams(
            collective_id=0, has_side_effects=True, vmem_limit_bytes=32 * 1024 * 1024),
        name="merge_tree",
    )(terminal.reshape(GOALS * 8, 128), goal_weight.reshape(GOALS * 8, 128), conduct.reshape(8, 128), active_count)


def solution(mesh):
    placed = (
        P("tm", None, "space", None, None),
        P(None, "space", None, None),
        P("space", None, None),
        P("tm"),
    )
    return jax.shard_map(
        shards, mesh=mesh, in_specs=placed, out_specs=P("tm", "space"), check_vma=False
    )
```

```python
import jax
import jax.numpy as jnp
from jax import lax
from jax.experimental import pallas as pl
from jax.experimental.pallas import tpu as pltpu
from jax.sharding import PartitionSpec as P

STEPS = 4
GOALS = 64
LAYERS = 8
NX_CHIPS = 4
N_TM = 4
CHUNKS = 8
GROUPS = 4
F32 = jnp.float32
BF16 = jnp.bfloat16


def split(x):
    high = x.astype(BF16)
    return high, (x - high.astype(F32)).astype(BF16)


def dot(a, b, dims):
    return lax.dot_general(a, b, (dims, ((), ())), preferred_element_type=F32)


def dot3(ah, al, bh, bl, dims=((1,), (0,))):
    return dot(ah, bh, dims) + (dot(ah, bl, dims) + dot(al, bh, dims))


NT = ((1,), (1,))


class Arrival:
    def __init__(self, sem, whole):
        self.sem, self.whole, self.done = sem, whole, False

    def wait(self):
        self.done = True
        pltpu.make_async_copy(self.whole, self.whole, self.sem).wait()


class Links:
    def __init__(self, send_sems, recv_sems):
        self.send_sems, self.recv_sems, self.sent, self.arrivals = send_sems, recv_sems, [], []

    def sending(self, whole):
        sem = self.send_sems.at[len(self.sent)]
        self.sent.append(Arrival(sem, whole))
        return sem

    def arrival(self, whole):
        arrival = Arrival(self.recv_sems.at[len(self.arrivals)], whole)
        self.arrivals.append(arrival)
        return arrival

    def group(self, copies, whole, send_sem=None):
        if send_sem is None:
            send_sem = self.sending(whole)
        arrival = self.arrival(whole)
        for src, dst, device in copies:
            self.copy(src, dst, device, send_sem, arrival)
        return arrival

    def copy(self, src, dst, device, send_sem, arrival):
        pltpu.make_async_remote_copy(
            src_ref=src, dst_ref=dst, send_sem=send_sem, recv_sem=arrival.sem,
            device_id=device, device_id_type=pl.DeviceIdType.MESH).start()

    def finish(self):
        for sent in self.sent:
            if not sent.done:
                sent.wait()


def rows(start, size):
    return pl.ds(pl.multiple_of(start, 8), size)


def kernel(n_space, term_ref, goal_ref, cond_ref, count_ref, out_ref,
           term_raw, goal_raw, in_sems, field, goal, halo, own, other, sh, sl,
           pe, pg, pc, ee, ge, cb, *rest):
    early_bufs, pair_bufs, cross_bufs = rest[:10], rest[10:20], rest[20:30]
    (s0f, s0h, s0l, zh, zl, s1h, s1l, ff, fh, fl, th, tl, wf, wh, wl,
           wb, hb, mh, ml, ph, pw, bs, land, send_sems, recv_sems) = rest[30:]
    s = lax.axis_index("space")
    t = lax.axis_index("tm")
    core = s % 2
    chip = s // 2
    cx = chip % NX_CHIPS
    cz = chip // NX_CHIPS
    n_z = n_space // (2 * NX_CHIPS)
    left = (lax.rem(s + n_space - 1, n_space), t)
    right = (lax.rem(s + 1, n_space), t)
    partner = (s + 1 - 2 * core, t)

    def y_peer(d):
        return lax.rem(t + d, N_TM)

    def x_peer(d):
        return lax.rem(cx + d, NX_CHIPS)

    def z_peer(d):
        return lax.rem(cz + d, n_z)

    def at_y(d):
        return (s, y_peer(d))

    def at_x(d):
        return ((cz * NX_CHIPS + x_peer(d)) * 2 + core, t)

    def at_z(d):
        return ((z_peer(d) * NX_CHIPS + cx) * 2 + core, t)

    peers = [left, right] + [at_y(d) for d in range(1, N_TM)] + [at_x(d) for d in range(1, NX_CHIPS)]
    peers += [at_z(d) for d in range(1, n_z)]
    barrier = pltpu.get_barrier_semaphore()
    for peer in peers:
        pl.semaphore_signal(barrier, inc=1, device_id=peer, device_id_type=pl.DeviceIdType.MESH)

    size = GOALS // CHUNKS
    loads = [pltpu.make_async_copy(term_ref, term_raw, in_sems.at[0]),
             pltpu.make_async_copy(goal_ref, goal_raw, in_sems.at[1])]
    for load in loads:
        load.start()
    lane = lax.broadcasted_iota(jnp.int32, (1, 128), 1)
    mask = (lane // (128 // LAYERS) < count_ref[0]).astype(F32)
    loads[0].wait()
    for y in range(8):
        for c in range(CHUNKS):
            field[0, c, y] = term_raw[pl.ds(c * size * 8 + y, size, stride=8), :] * mask
    pl.semaphore_wait(barrier, len(peers))

    links = Links(send_sems, recv_sems)

    halo_sem = links.sending(halo)
    spread_sem = links.sending(own.at[:, pl.ds(0, N_TM - 1)])
    share_sem = links.sending(own)

    def send_halo(k, c):
        return links.group([(field.at[k, c], halo.at[k, c, 0], right), (field.at[k, c], halo.at[k, c, 1], left)],
                           halo.at[k, c], halo_sem)

    def offsets(count):
        return sorted(range(1, count), key=lambda d: -min(d, count - d))

    def scatter(src, base, land, length, peer, at, count):
        return links.group([(src.at[rows(base + peer(d) * length, length)], land.at[d - 1], at(d))
                            for d in offsets(count)], land)

    def reduced(src, base, land, length, arrival, place):
        total = src[rows(base + place * length, length)]
        arrival.wait()
        for d in range(land.shape[0]):
            total = total + land[d]
        return total

    def gather(src, dst, base, length, place, at, count):
        return links.group([(src, dst.at[rows(base + place * length, length)], at(d)) for d in offsets(count)],
                           dst.at[pl.ds(base, (count - 1) * length)])

    def stage1(src, bufs):
        landx, landy = bufs[:2]
        half = src.shape[0] // 2
        return (scatter(src, 0, landx, half // 4, x_peer, at_x, NX_CHIPS),
                scatter(src, half, landy, half // 4, y_peer, at_y, N_TM))

    def stage2(src, bufs, copies):
        landx, landy, qx, qy, landx2, landy2 = bufs[:6]
        half = src.shape[0] // 2
        qx[...] = reduced(src, 0, landx, half // 4, copies[0], cx)
        first = scatter(qx, 0, landx2, half // 16, y_peer, at_y, N_TM)
        qy[...] = reduced(src, half, landy, half // 4, copies[1], t)
        return first, scatter(qy, 0, landy2, half // 16, x_peer, at_x, NX_CHIPS)

    def stage3(bufs, copies):
        qx, qy, landx2, landy2, q, land = bufs[2:8]
        length = qx.shape[0] // 4
        q[pl.ds(0, length)] = reduced(qx, 0, landx2, length, copies[0], t)
        q[pl.ds(length, length)] = reduced(qy, 0, landy2, length, copies[1], cx)
        if q.shape[0] > 2 * length:
            q[pl.ds(2 * length, q.shape[0] - 2 * length)] = jnp.zeros((q.shape[0] - 2 * length, 128), F32)
        return scatter(q, 0, land, q.shape[0] // n_z, z_peer, at_z, n_z)

    def back1(bufs, copies):
        q, land, full = bufs[6:9]
        length = q.shape[0] // n_z
        full[rows(cz * length, length)] = reduced(q, 0, land, length, copies, cz)
        return gather(full.at[rows(cz * length, length)], full, 0, length, cz, at_z, n_z)

    def back2(bufs, copies):
        full = bufs[8]
        qx, qy = bufs[9].at[0], bufs[9].at[1]
        copies.wait()
        length = qx.shape[0] // 4
        first = gather(full.at[pl.ds(0, length)], qx, 0, length, t, at_y, N_TM)
        second = gather(full.at[pl.ds(length, length)], qy, 0, length, cx, at_x, NX_CHIPS)
        qx[rows(t * length, length)] = full[pl.ds(0, length)]
        qy[rows(cx * length, length)] = full[pl.ds(length, length)]
        return first, second

    def back3(bufs, copies, dst):
        qx, qy = bufs[9].at[0], bufs[9].at[1]
        length = qx.shape[0]
        copies[0].wait()
        first = gather(qx, dst, 0, length, cx, at_x, NX_CHIPS)
        copies[1].wait()
        second = gather(qy, dst, 4 * length, length, t, at_y, N_TM)
        dst[rows(cx * length, length)] = qx[...]
        dst[rows(4 * length + t * length, length)] = qy[...]
        return first, second

    has_left = jnp.where(s > 0, 1.0, 0.0).astype(F32)
    has_right = jnp.where(s < n_space - 1, 1.0, 0.0).astype(F32)
    inner_lo = (lane > 0).astype(F32)
    inner_hi = (lane < 127).astype(F32)
    halos = {(0, c): send_halo(0, c) for c in range(CHUNKS)}
    loads[1].wait()
    for y in range(8):
        for c in range(CHUNKS):
            goal[c, y] = goal_raw[pl.ds(c * size * 8 + y, size, stride=8), :] * mask
    final_step, each = STEPS - 1, CHUNKS // GROUPS
    spread = [links.arrival(own.at[k, pl.ds(0, N_TM - 1)]) for k in range(final_step)]
    last_spread = [links.arrival(own.at[final_step, pl.ds(0, N_TM - 1), pl.ds(g * each, each)])
                   for g in range(GROUPS)]

    def absorb(ref, base, k, c, count):
        for yy in range(2):
            for b in range(N_TM):
                high, low = split(ref[k, b, pl.ds(c, count), yy].reshape(count * size, 128))
                place = pl.ds(k * GOALS + c * size, count * size)
                sh[b, place, pl.ds(base + yy * 128, 128)] = high
                sl[b, place, pl.ds(base + yy * 128, 128)] = low

    def share(arrival, k, c, count):
        arrival.wait()
        some = (k, slice(None), pl.ds(c, count))
        return links.group([(own.at[some], other.at[some], partner)], other.at[some], share_sem)

    shared = {}
    for k in range(STEPS):
        for c in range(CHUNKS):
            halos[k, c].wait()
            for y in range(8):
                here = field[k, c, y]
                total = halo[k, c, 0, y] * has_left + halo[k, c, 1, y] * has_right
                if y > 0:
                    total = total + field[k, c, y - 1]
                if y < 7:
                    total = total + field[k, c, y + 1]
                total = total + pltpu.roll(here, 1, 1) * inner_lo + pltpu.roll(here, 127, 1) * inner_hi
                kappa = cond_ref[pl.ds(y, 1), :]
                field[k + 1, c, y] = mask * (here + kappa * (total - 6.0 * here)) + goal[c, y]
            if k + 1 < STEPS:
                halos[k + 1, c] = send_halo(k + 1, c)
            for d in (2, 1, 3):
                links.copy(field.at[k + 1, c, pl.ds(2 * y_peer(d), 2)], own.at[k, t, c], at_y(d), spread_sem,
                           spread[k] if k < final_step else last_spread[c // each])
            own[k, t, c] = field[k + 1, c, pl.ds(2 * t, 2)]
        if k > 0:
            shared[k - 1] = share(spread[k - 1], k - 1, 0, CHUNKS)
            absorb(own, 0, k - 1, 0, CHUNKS)
        if k > 1:
            shared[k - 2].wait()
            absorb(other, 256, k - 2, 0, CHUNKS)
    shared[final_step - 1].wait()
    absorb(other, 256, final_step - 1, 0, CHUNKS)

    lower, upper = 2 * core, 2 * core + 1
    first, second = pl.ds(0, 128), pl.ds(128, 128)

    def both(ref, i, j):
        return jnp.concatenate([ref[i, first], ref[j, first]], 0)

    def early(i, j, k):
        return dot3(sh[i, first], sl[i, first], both(sh, j, k), both(sl, j, k), NT)

    g = early(lower, lower, upper)
    pe[pl.ds(0, 128)] = g[:, :128]
    pe[pl.ds(128, 128)] = g[:, 128:]
    g = dot3(sh[upper, first], sl[upper, first], sh[upper, first], sl[upper, first], NT)
    pe[pl.ds(256, 128)] = g
    g = early(core, 2, 3)
    pe[pl.ds(384, 128)] = g[:, :128]
    pg[pl.ds(896, 128)] = g[:, 128:]
    e1 = stage1(pe, early_bufs)
    last_shared = []
    for g in range(GROUPS):
        last_shared.append(share(last_spread[g], final_step, g * each, each))
        absorb(own, 0, final_step, g * each, each)
    for g in range(GROUPS):
        last_shared[g].wait()
        absorb(other, 256, final_step, g * each, each)

    e2 = stage2(pe, early_bufs, e1)

    def put(ref, n, value):
        ref[pl.ds(128 * n, 128)] = value

    def late(n, i):
        g = dot3(sh[i, second], sl[i, second], sh[i], sl[i], NT)
        put(pg, n, g[:, :128])
        put(pg, n + 1, g[:, 128:])

    def mixed(ref, n, i, j):
        g = dot3(sh[i], sl[i], sh[j], sl[j], NT)
        put(ref, n, g[:128, 128:])
        put(ref, n + 1, g[128:, :128])
        put(ref, n + 2, g[128:, 128:])

    late(0, lower)
    mixed(pg, 2, lower, upper)
    late(5, upper)
    g1 = stage1(pg, pair_bufs)
    mixed(pc, 0, core, 2)
    mixed(pc, 3, core, 3)

    cmat = cb.at[core, pl.ds(0, 768)]
    c1 = stage1(pc, cross_bufs)
    e3 = stage3(early_bufs, e2)
    g2 = stage2(pg, pair_bufs, g1)
    c2 = stage2(pc, cross_bufs, c1)
    e4 = back1(early_bufs, e3)
    g3 = stage3(pair_bufs, g2)
    c3 = stage3(cross_bufs, c2)
    e5 = back2(early_bufs, e4)
    g4 = back1(pair_bufs, g3)
    c4 = back1(cross_bufs, c3)
    e6 = back3(early_bufs, e5, ee)
    g5 = back2(pair_bufs, g4)
    c5 = back2(cross_bufs, c4)
    g6 = back3(pair_bufs, g5, ge)
    c6 = back3(cross_bufs, c5, cmat)
    for arrival in e6:
        arrival.wait()
    for arrival in g6:
        arrival.wait()

    identity = (lax.broadcasted_iota(jnp.int32, (256, 256), 0)
                == lax.broadcasted_iota(jnp.int32, (256, 256), 1)).astype(F32)
    halves = (pl.ds(0, 256), pl.ds(256, 256))

    def square(upper_left, lower_left, lower_right):
        top = jnp.concatenate([upper_left, lower_left.T], 1)
        return jnp.concatenate([top, jnp.concatenate([lower_left, lower_right], 1)], 0)

    def tile(ref, n):
        return ref[pl.ds(128 * n, 128)]

    def put_s0(i, j, value):
        s0f[halves[i], halves[j]] = value
        s0h[halves[i], halves[j]], s0l[halves[i], halves[j]] = split(value)

    def weights(g00, g01, g11, trace):
        energy = trace / 512.0 + 1e-6
        inverse = 1.0 / energy
        upper, lower_, across = g00 * inverse - identity, g11 * inverse - identity, g01 * inverse
        put_s0(0, 0, upper)
        put_s0(1, 1, lower_)
        put_s0(0, 1, across)
        put_s0(1, 0, across.T)
        norm2 = jnp.sum(upper * upper + lower_ * lower_ + 2.0 * (across * across)) + 1e-6
        scale = 1.0 / jnp.sqrt(norm2)
        for r in halves:
            zh[r], zl[r] = split(dot3(s0h[r], s0l[r], s0h[...], s0l[...]))
        folded = None
        for r in halves:
            s1 = (1.5 * scale) * s0f[r] - (0.5 * scale / norm2) * dot3(s0h[r], s0l[r], zh[...], zl[...])
            s1h[r], s1l[r] = split(s1)
            folded = s1 if folded is None else folded + s1
        ff[...] = folded
        fh[...], fl[...] = split(folded)
        th[...], tl[...] = split(dot3(fh[...], fl[...], s1h[...], s1l[...]))
        u = dot3(th[...], tl[...], s1h[...], s1l[...])
        w = (jnp.concatenate([identity, identity], 1) + 1.5 * ff[...] - 0.5 * u) * (0.5 / 2.0 ** 0.5)
        wf[...] = w
        wh[...], wl[...] = split(w)
        return energy

    def kept_part(energy):
        gw = wf[...] + dot3(wh[...], wl[...], s0h[...], s0l[...])
        ff[...] = gw
        kept = energy * jnp.sum(wf[...] * gw)
        alpha = jnp.sqrt(energy * 256.0 / (kept + 1e-6))
        return alpha, alpha * alpha * kept

    trace = jnp.sum((tile(ee, 0) + tile(ge, 1) + tile(ee, 2) + tile(ge, 6)) * identity[:128, :128])
    energy = weights(
        square(tile(ee, 0), tile(ge, 0), tile(ge, 1)),
        jnp.concatenate([jnp.concatenate([tile(ee, 1), tile(ge, 2)], 1),
                         jnp.concatenate([tile(ge, 3), tile(ge, 4)], 1)], 0),
        square(tile(ee, 2), tile(ge, 5), tile(ge, 6)), trace)
    wb[core] = wf[...]
    send_w = links.group([(wb.at[core], wb.at[core], partner)], wb.at[core])
    for arrival in c6:
        arrival.wait()
    cb[core, pl.ds(768, 128)] = tile(ee, 3)
    cb[core, pl.ds(896, 128)] = tile(ge, 7)
    send_c = links.group([(cb.at[core], cb.at[core], partner)], cb.at[core])
    alpha, trace = kept_part(energy)
    fh[...], fl[...] = split(ff[...])
    hb[core, pl.ds(0, 256)] = (energy * alpha * alpha) * dot3(fh[...], fl[...], wh[...], wl[...], NT)
    hb[core, pl.ds(256, 8)] = jnp.full((8, 256), alpha, F32)
    hb[core, pl.ds(264, 8)] = jnp.full((8, 256), trace, F32)
    send_h = links.group([(hb.at[core], hb.at[core], partner)], hb.at[core])
    send_w.wait()

    send_c.wait()
    wh[...], wl[...] = split(wb[1])
    for i in range(2):
        c_rows = jnp.concatenate([jnp.concatenate([cb[i, pl.ds(128 * n, 128)] for n in order], 1)
                                  for order in ((6, 0, 7, 3), (1, 2, 4, 5))], 0)
        ch, cl = split(c_rows)
        ph[halves[i]], pw[halves[i]] = split(dot3(ch, cl, wh[...], wl[...], NT))
    wh[...], wl[...] = split(wb[0])
    cross = dot3(wh[...], wl[...], ph[...], pw[...])
    send_h.wait()
    alphas = [hb[p, pl.ds(256, 1)] for p in range(2)]
    for p in range(2):
        ah, al = split(wb[p])
        terms = [dot3(ah[:, 256 * i:256 * i + 256], al[:, 256 * i:256 * i + 256],
                      sh[2 * p + i, :, pl.ds(0, 256)], sl[2 * p + i, :, pl.ds(0, 256)]) for i in range(2)]
        mh[halves[p]], ml[halves[p]] = split((terms[0] + terms[1]) * alphas[p])
    energy = weights(hb[0, pl.ds(0, 256)], cross * (alphas[0] * alphas[1]), hb[1, pl.ds(0, 256)],
                     jnp.sum(hb[0, pl.ds(264, 1), pl.ds(0, 1)] + hb[1, pl.ds(264, 1), pl.ds(0, 1)]))
    bs[...] = dot3(wh[...], wl[...], mh[...], ml[...])
    columns = pl.ds(pl.multiple_of(t * 256, 256), 256)
    final = links.group([(bs.at[rows(y_peer(d) * 64, 64)], land.at[:, columns], at_y(d)) for d in (2, 1, 3)],
                        land.at[:, pl.ds(0, 768)])
    land[:, columns] = bs[rows(t * 64, 64)]
    alpha = kept_part(energy)[0]
    for sent in links.sent[:-1]:
        sent.wait()
    final.wait()
    out_ref[...] = alpha * land[...]
    links.finish()


def shards(terminal, goal_weight, conduct, active_count):
    n_space = lax.axis_size("space")
    n_z = n_space // (2 * NX_CHIPS)

    size = GOALS // CHUNKS

    def f(*shape):
        return pltpu.VMEM(shape, F32)

    def h(*shape):
        return pltpu.VMEM(shape, BF16)

    def stages(length):
        one, two = length // 8, length // 32
        pad = -(-2 * two // (8 * n_z)) * 8 * n_z
        return [f(3, one, 128), f(3, one, 128), f(one, 128), f(one, 128), f(3, two, 128), f(3, two, 128),
                f(pad, 128), f(n_z - 1, pad // n_z, 128), f(pad, 128), f(2, one, 128)]

    scratch = [
        f(GOALS * 8, 128), f(GOALS * 8, 128), pltpu.SemaphoreType.DMA((2,)),
        f(STEPS + 1, CHUNKS, 8, size, 128), f(CHUNKS, 8, size, 128),
        f(STEPS, CHUNKS, 2, 8, size, 128),
        f(STEPS, N_TM, CHUNKS, 2, size, 128), f(STEPS, N_TM, CHUNKS, 2, size, 128), h(4, 256, 512), h(4, 256, 512),
        f(512, 128), f(1024, 128), f(768, 128), f(512, 128), f(1024, 128), f(2, 1024, 128),
        *stages(512), *stages(1024), *stages(768),
        f(512, 512), h(512, 512), h(512, 512), h(512, 512), h(512, 512), h(512, 512), h(512, 512),
        f(256, 512), h(256, 512), h(256, 512), h(256, 512), h(256, 512), f(256, 512), h(256, 512), h(256, 512),
        f(2, 256, 512), f(2, 272, 256), h(512, 256), h(512, 256), h(512, 256), h(512, 256), f(256, 256), f(64, 1024),
        pltpu.SemaphoreType.DMA((37,)), pltpu.SemaphoreType.DMA((80,)),
    ]
    vmem = pl.BlockSpec(memory_space=pltpu.VMEM)
    place = pl.BlockSpec(memory_space=pl.ANY)

    def body(*refs):
        kernel(n_space, *refs)

    return pl.pallas_call(
        body,
        out_shape=jax.ShapeDtypeStruct((256 // N_TM, 1024), F32),
        in_specs=[place, place, vmem, pl.BlockSpec(memory_space=pltpu.SMEM)],
        out_specs=vmem,
        scratch_shapes=scratch,
        compiler_params=pltpu.CompilerParams(
            collective_id=0, has_side_effects=True, vmem_limit_bytes=32 * 1024 * 1024),
        name="merge_tree",
    )(terminal.reshape(GOALS * 8, 128), goal_weight.reshape(GOALS * 8, 128), conduct.reshape(8, 128), active_count)


def solution(mesh):
    placed = (
        P("tm", None, "space", None, None),
        P(None, "space", None, None),
        P("space", None, None),
        P("tm"),
    )
    return jax.shard_map(
        shards, mesh=mesh, in_specs=placed, out_specs=P("tm", "space"), check_vma=False
    )
```
